256 devices in a mesh: docs: 64 (over z, y, x_lo), query: 4 (over x_hi, core).
Axes of the slice: x: 4 (x_hi: 2, x_lo: 2; x = x_hi * 2 + x_lo), y: 4, z: 8, core: 2. Of those that a mesh axis runs over, the one named last changes fastest.
Arguments:
- activations: bfloat16 [4, 8192, 4096], P('query', 'docs'), may hold values from -6 to 6
- out_grads: bfloat16 [4, 8192, 14336], P('query', 'docs'), may hold values from -6 to 6
- proj_in: bfloat16 [4096, 64], replicated, may hold values from -0.09375 to 0.09375
- proj_out: bfloat16 [14336, 64], replicated, may hold values from -0.046875 to 0.046875
- panels: bfloat16 [512, 4096], P('query'), may hold values from -0.09375 to 0.09375
- lengths: int32 [4, 64, 64], P('query', 'docs'), may hold values from 1 to 4, 128 in all within a row
- piece_owner: int32 [4, 64, 64], P('query', 'docs'), may hold values from 0 to 63, each once within a row
- doc_slot: int32 [4, 64, 64], P('query', None, 'docs'), may hold values from 0 to 7
- panel_order: int32 [64, 4], P('docs'), may hold values from 0 to 3, each once within a row
Outputs:
- scores: float32 [4, 512, 512], P('query', 'docs')
The draws below stay inside these ranges and needn't reach their ends.
Inputs may be any that keep to these rules, and one draw needn't show every extreme that they name: `lengths`: each row sums to 128; the largest entry of every row is exactly 4. `piece_owner`: each row is a permutation of the 64 owners. `panel_order`: each row is a permutation of the 4 panels.
All inputs are finite; a program needn't handle non-finite values.
Results may differ from the reference program's by a relative error of at most 0.0057.
Values may be sent and summed in bfloat16 or wider, within the bound.
No kernel may reach another device: no remote copies, remote signals or barrier semaphores. Data moves between devices by JAX's collectives and lax.ppermute only.
A program may use at most 64 MiB of HBM per device.

```python
import math
import jax
import jax.numpy as jnp
import numpy as np
from jax import lax

D = 4096
FF = 14336
R = 64
PANEL = 128
TOK_DEV = 128
DOC_OWN = 8
CAP = 4
TOKENS = 8192
QUERIES = 512
N_DOCS = 64
N_QUERY = 4


def plant(array, own_key, least, top_value):
    shape = array.shape
    index_at = [jax.random.randint(jax.random.fold_in(own_key, axis), (), 0, shape[axis]) for axis in range(len(shape))]
    array = array.at[tuple(index_at)].set(least)
    longest = shape.index(max(shape))
    index_at[longest] = (index_at[longest] + 1) % shape[longest]
    return array.at[tuple(index_at)].set(top_value)


def levels(rng, shape, pieces, smallest, high):
    level, own = 1.0, jax.random.fold_in(rng, 6)
    for axis_at, parts in pieces:
        steps = jnp.exp(jax.random.uniform(jax.random.fold_in(own, axis_at), (parts,), jnp.float32, smallest / len(pieces), high / len(pieces)))
        level = level * jnp.repeat(steps, shape[axis_at] // parts).reshape([-1 if axis == axis_at else 1 for axis in range(len(shape))])
    return level


def split_up(amount, total, bound, slope):
    loads = [(1 << 20) // math.isqrt(grade ** slope) + 1 for grade in range(2, amount + 1)]
    rest, holding = total - bound - (amount - 1), [1] * (amount - 1)
    while rest > 0:
        movable = [i for i in range(amount - 1) if holding[i] < bound]
        mass, budget = sum([loads[i] for i in movable]), rest
        for i in movable:
            addition = min(bound - holding[i], max(1, budget * loads[i] // mass), rest)
            holding[i] = holding[i] + addition
            rest = rest - addition
    return np.array([bound] + holding)


def uneven(own_key, count, total, most, skew):
    if count == 2:
        one = jax.random.randint(own_key, (), max(1, total - most), min(most, total - 1) + 1)
        return jnp.stack([one, total - one])
    sizes = jnp.asarray(split_up(count, total, most, skew), jnp.int32)
    pairs = (count - 1) // 2
    donor, sink = sizes[1:1 + 2 * pairs:2], sizes[2:2 + 2 * pairs:2]
    room = jnp.minimum(donor - 1, most - sink)
    shifted = jax.random.randint(jax.random.fold_in(own_key, 1), (pairs,), 0, 1 << 20) % (room + 1)
    sizes = sizes.at[1:1 + 2 * pairs:2].set(donor - shifted).at[2:2 + 2 * pairs:2].set(sink + shifted)
    return sizes[jax.random.permutation(jax.random.fold_in(own_key, 2), count)]


def gaussian(own_key, shape, spread, most, split=(), kind=jnp.bfloat16):
    entries = spread * jax.random.normal(own_key, shape, jnp.float32)
    if split:
        entries = entries * levels(own_key, shape, split, -0.22, 0.18)
    return jnp.clip(entries, -most, most).astype(kind)


def setup_inputs(seed: int = 0) -> dict:
    seeds = jax.random.split(jax.random.key(seed), 10)
    activations = gaussian(seeds[0], (N_QUERY, TOKENS, D), 1.0, 6.0, ((0, 4), (1, 64)))
    out_grads = gaussian(seeds[1], (N_QUERY, TOKENS, FF), 1.0, 6.0, ((0, 4), (1, 64)))
    proj_in = gaussian(seeds[2], (D, R), D ** -0.5, 0.09375)
    proj_out = gaussian(seeds[3], (FF, R), FF ** -0.5, 0.046875)
    panels = gaussian(seeds[4], (QUERIES, R * R), (R * R) ** -0.5, 0.09375, ((0, 4),))
    lengths = jax.vmap(lambda own: uneven(own, N_DOCS, TOK_DEV, CAP, 2))(jax.random.split(seeds[5], N_QUERY * N_DOCS)).reshape((N_QUERY, N_DOCS, N_DOCS)).astype(jnp.int32)
    piece_owner = jax.vmap(lambda own: jax.random.permutation(own, N_DOCS))(jax.random.split(seeds[6], N_QUERY * N_DOCS)).reshape((N_QUERY, N_DOCS, N_DOCS)).astype(jnp.int32)
    doc_slot = plant(jax.random.randint(seeds[7], (N_QUERY, N_DOCS, N_DOCS), 0, DOC_OWN), jax.random.fold_in(seeds[7], 1), 0, DOC_OWN - 1).astype(jnp.int32)
    panel_order = jax.vmap(lambda own: jax.random.permutation(own, N_QUERY))(jax.random.split(seeds[8], N_DOCS)).reshape((N_DOCS, N_QUERY)).astype(jnp.int32)
    return {"activations": activations, "out_grads": out_grads, "proj_in": proj_in, "proj_out": proj_out, "panels": panels, "lengths": lengths, "piece_owner": piece_owner, "doc_slot": doc_slot, "panel_order": panel_order}


def group_grads(acts, grads, proj_in, proj_out, piece_len, piece_owner, slot_map):
    act_rows = acts.reshape(N_DOCS, TOK_DEV, D)
    grad_rows = grads.reshape(N_DOCS, TOK_DEV, FF)

    def one_source(total, inputs):
        act_block, grad_block, lens, owners, slots = inputs
        act_low = jnp.dot(act_block, proj_in, preferred_element_type=jnp.float32).astype(jnp.bfloat16)
        grad_low = jnp.dot(grad_block, proj_out, preferred_element_type=jnp.float32).astype(jnp.bfloat16)
        outer = grad_low.astype(jnp.float32)[:, :, None] * act_low.astype(jnp.float32)[:, None, :]
        outer = outer.reshape(TOK_DEV, R * R).astype(jnp.bfloat16)
        ends = jnp.cumsum(lens).astype(jnp.int32)
        rows_at = jnp.arange(TOK_DEV, dtype=jnp.int32)
        piece = jnp.sum((rows_at[:, None] >= ends[None, :]).astype(jnp.int32), axis=1).astype(jnp.int32)
        owner = owners[piece].astype(jnp.int32)
        slot = slots[owner].astype(jnp.int32)
        document = (owner * DOC_OWN + slot).astype(jnp.int32)
        total = total.at[document].add(outer.astype(jnp.float32))
        return total, None

    start_total = jnp.zeros((N_DOCS * DOC_OWN, R * R), jnp.float32)
    total, _ = lax.scan(one_source, start_total, (act_rows, grad_rows, piece_len, piece_owner, slot_map))
    return total.astype(jnp.bfloat16)


def reference(activations, out_grads, proj_in, proj_out, panels, lengths, piece_owner, doc_slot, panel_order):
    results = []
    order_index = jnp.broadcast_to(panel_order.astype(jnp.int32)[:, None, :, None],
                                   (N_DOCS, DOC_OWN, N_QUERY, PANEL))
    for group in range(N_QUERY):
        grads_now = group_grads(activations[group], out_grads[group], proj_in, proj_out,
                                lengths[group], piece_owner[group], doc_slot[group])
        full = lax.dot_general(grads_now, panels, (((1,), (1,)), ((), ())),
                               preferred_element_type=jnp.float32)
        full = full.reshape(N_DOCS, DOC_OWN, N_QUERY, PANEL)
        picked = jnp.take_along_axis(full, order_index, axis=2)
        results.append(picked.reshape(N_DOCS * DOC_OWN, N_QUERY * PANEL))
    return jnp.stack(results)
```

```python
import jax
import jax.numpy as jnp
from jax import lax
from jax.experimental import pallas as pl
from jax.experimental.pallas import tpu as pltpu
from jax.sharding import PartitionSpec as P

DOC_OWN = 8
R = 64
CAP = 4
DOCS = 64
TOK = 128
ROWS = DOCS * CAP
PANEL = 128
QUART = PANEL // 4
NT = (((1,), (1,)), ((), ()))


def column_chunks(width, step):
    return [(at, min(step, width - at)) for at in range(0, width, step)]


def project_kernel(act_hbm, grad_hbm, win_hbm, wout_hbm, len_ref, own_ref, slot_ref,
                   rows_ref, member_ref, act_v, grad_v, win_v, wout_v, sems):
    jobs = []
    for x_hbm, w_hbm, x_v, w_v in (
        (act_hbm, win_hbm, act_v, win_v),
        (grad_hbm, wout_hbm, grad_v, wout_v),
    ):
        for at, size in column_chunks(x_hbm.shape[-1], 2048):
            cols = pl.ds(at, size)
            n = 2 * len(jobs)
            copies = (
                pltpu.make_async_copy(w_hbm.at[:, cols], w_v.at[:, cols], sems.at[n]),
                pltpu.make_async_copy(x_hbm.at[0, :, cols], x_v.at[:, cols], sems.at[n + 1]),
            )
            for copy in copies:
                copy.start()
            jobs.append((copies, x_v, w_v, cols))

    row = lax.broadcasted_iota(jnp.int32, (ROWS, DOCS), 0)
    piece = lax.broadcasted_iota(jnp.int32, (ROWS, DOCS), 1).astype(jnp.float32)
    lens = len_ref[...].astype(jnp.float32)
    chosen = own_ref[...] == (row >> 2)
    place = jnp.sum(jnp.where(chosen, piece, 0.0), axis=1, keepdims=True)
    amount = jnp.sum(jnp.where(chosen, lens, 0.0), axis=1, keepdims=True)
    offset = jnp.sum(jnp.where(piece < place, lens, 0.0), axis=1, keepdims=True)
    within = (lax.broadcasted_iota(jnp.int32, (ROWS, TOK), 0) & (CAP - 1)).astype(jnp.float32)
    token = lax.broadcasted_iota(jnp.int32, (ROWS, TOK), 1).astype(jnp.float32)
    take = jnp.where((token == offset + within) & (within < amount), 1.0, 0.0)
    take = take.astype(jnp.bfloat16)

    doc = lax.broadcasted_iota(jnp.int32, (DOC_OWN, DOCS), 0)
    mine = jnp.where(slot_ref[...] == doc, 1.0, 0.0).astype(jnp.bfloat16)
    source = lax.broadcasted_iota(jnp.int32, (DOCS, ROWS), 0)
    spread = jnp.where((lax.broadcasted_iota(jnp.int32, (DOCS, ROWS), 1) >> 2) == source, 1.0, 0.0)
    member_ref[...] = jnp.dot(mine, spread.astype(jnp.bfloat16), preferred_element_type=jnp.float32)

    low = {}
    for copies, x_v, w_v, cols in jobs:
        for copy in copies:
            copy.wait()
        part = lax.dot_general(x_v[:, cols], w_v[:, cols], NT, preferred_element_type=jnp.float32)
        low[id(x_v)] = part if id(x_v) not in low else low[id(x_v)] + part
    rows = jnp.concatenate([low[id(grad_v)], low[id(act_v)]], axis=1).astype(jnp.bfloat16)
    rows_ref[...] = jnp.dot(take, rows, preferred_element_type=jnp.float32).astype(jnp.bfloat16)


def project(activations, out_grads, proj_in, proj_out, lengths, piece_owner, slots):
    width_in, width_out = activations.shape[-1], out_grads.shape[-1]
    chunks = len(column_chunks(width_in, 2048)) + len(column_chunks(width_out, 2048))
    hbm = pl.BlockSpec(memory_space=pltpu.HBM)
    vmem = pl.BlockSpec(memory_space=pltpu.VMEM)
    return pl.pallas_call(
        project_kernel,
        out_shape=(
            jax.ShapeDtypeStruct((ROWS, 2 * R), jnp.bfloat16),
            jax.ShapeDtypeStruct((DOC_OWN, ROWS), jnp.float32),
        ),
        in_specs=[hbm] * 4 + [vmem] * 3,
        out_specs=(vmem, vmem),
        scratch_shapes=[
            pltpu.VMEM((TOK, width_in), jnp.bfloat16),
            pltpu.VMEM((TOK, width_out), jnp.bfloat16),
            pltpu.VMEM((R, width_in), jnp.bfloat16),
            pltpu.VMEM((R, width_out), jnp.bfloat16),
            pltpu.SemaphoreType.DMA((2 * chunks,)),
        ],
        compiler_params=pltpu.CompilerParams(vmem_limit_bytes=56 << 20),
        cost_estimate=pl.CostEstimate(
            flops=2 * TOK * (width_in + width_out) * R,
            bytes_accessed=2 * (TOK + R) * (width_in + width_out),
            transcendentals=0,
        ),
        name="project",
    )(activations, out_grads, proj_in.T, proj_out.T, lengths, piece_owner, slots)


def score_kernel(place_ref, rows_ref, member_ref, *refs):
    panel_refs, out_ref = refs[:-1], refs[-1]
    rows = rows_ref[...]
    eye = (lax.broadcasted_iota(jnp.int32, (2 * R, 2 * R), 0)
           == lax.broadcasted_iota(jnp.int32, (2 * R, 2 * R), 1))
    eye = jnp.where(eye, 1.0, 0.0).astype(jnp.bfloat16)
    turned = lax.dot_general(eye, rows, NT, preferred_element_type=jnp.float32)
    masked = turned[:R][:, None, :] * member_ref[...][None]
    masked = masked.reshape(R * DOC_OWN, ROWS).astype(jnp.bfloat16)
    wide = rows.astype(jnp.float32)
    lane = lax.broadcasted_iota(jnp.int32, (ROWS, 2 * R), 1)
    twice = jnp.where(lane < R, pltpu.roll(wide, R, 1), wide).astype(jnp.bfloat16)
    grads = jnp.dot(masked, twice, preferred_element_type=jnp.float32)
    grads = grads.reshape(R, DOC_OWN, 2 * R)
    low_half = lax.broadcasted_iota(jnp.int32, (DOC_OWN, 2 * R), 1) < R
    grads = jnp.concatenate(
        [jnp.where(low_half, grads[2 * i], grads[2 * i + 1]) for i in range(R // 2)], axis=1
    ).astype(jnp.bfloat16)

    def against(ref):
        return lax.dot_general(ref[...], grads, NT, preferred_element_type=jnp.float32)

    def put(kth, block):
        at = pl.multiple_of(place_ref[kth] * PANEL, PANEL)
        out_ref[0, :, pl.ds(at, PANEL)] = jnp.transpose(block)

    put(0, against(panel_refs[0]))
    put(1, against(panel_refs[1]))
    mine = place_ref[4]
    for kth in (2, 3):
        parts = [against(ref) for ref in panel_refs[4 * kth - 6:4 * kth - 2]]
        ordered = []
        for quarter in range(4):
            turn = mine ^ quarter
            ordered.append(jnp.where(turn == 0, parts[0], jnp.where(
                turn == 1, parts[1], jnp.where(turn == 2, parts[2], parts[3]))))
        put(kth, jnp.concatenate(ordered, axis=0))


def score(place, arrived, member, panels):
    smem = pl.BlockSpec(memory_space=pltpu.SMEM)
    vmem = pl.BlockSpec(memory_space=pltpu.VMEM)
    return pl.pallas_call(
        score_kernel,
        out_shape=jax.ShapeDtypeStruct((1, DOC_OWN, 4 * PANEL), jnp.float32),
        in_specs=[smem] + [vmem] * (2 + len(panels)),
        out_specs=vmem,
        compiler_params=pltpu.CompilerParams(vmem_limit_bytes=56 << 20),
        name="score",
    )(place, arrived, member, *panels)


def hop(fn):
    pairs = []
    for z in range(8):
        for y in range(4):
            for x in range(4):
                for core in range(2):
                    at = []
                    for c in ((z, y, x, core), fn(z, y, x, core)):
                        at.append((((c[0] * 4 + c[1]) * 2 + c[2] % 2) * 2 + c[2] // 2) * 2 + c[3])
                    pairs.append(tuple(at))
    return pairs


TO_CORE = hop(lambda z, y, x, core: (z, y, x, 1 - core))
TO_CROSS = hop(lambda z, y, x, core: (z, y, 3 - x, core))
TO_X = hop(lambda z, y, x, core: (z, y, x ^ 1, core))
TO_Y = hop(lambda z, y, x, core: (z, y ^ 1, x, core))
TO_Z = hop(lambda z, y, x, core: (z ^ 1, y, x, core))


def send(value, pairs):
    return lax.ppermute(value, ("docs", "query"), pairs)


def shards(
    activations, out_grads, proj_in, proj_out, panels, lengths, piece_owner, doc_slot, panel_order
):
    docs_at = lax.axis_index("docs")
    query_at = lax.axis_index("query")
    quarter = (docs_at & 1) ^ (2 * ((docs_at >> 1) & 1)) ^ (3 * ((docs_at >> 3) & 1))

    across = send(lax.dynamic_slice_in_dim(panels, (quarter ^ 1) * QUART, QUART, 0), TO_CROSS)
    packed, member = project(
        activations, out_grads, proj_in, proj_out,
        lengths[0], piece_owner[0], doc_slot[0].reshape(1, DOCS),
    )
    across, panels, _ = lax.optimization_barrier((across, panels, packed))
    beside = send(panels, TO_CORE)
    parts = [across] + [send(across, to) for to in (TO_X, TO_Y, TO_Z)]
    parts_beside = [send(part, TO_CORE) for part in parts]
    arrived = lax.all_to_all(
        packed.reshape(DOCS, CAP, 2 * R), "docs", split_axis=0, concat_axis=0, tiled=True
    ).reshape(ROWS, 2 * R)

    order = panel_order[0]
    held = query_at ^ jnp.arange(4, dtype=jnp.int32)
    place = jnp.sum((order[None, :] == held[:, None]) * jnp.arange(4, dtype=jnp.int32), axis=1)
    place = jnp.concatenate([place.astype(jnp.int32), quarter.reshape(1).astype(jnp.int32)])
    return score(place, arrived, member, [panels, beside] + parts + parts_beside)


def solution(mesh):
    placed = (
        P("query", "docs", None),
        P("query", "docs", None),
        P(),
        P(),
        P("query", None),
        P("query", "docs", None),
        P("query", "docs", None),
        P("query", None, "docs"),
        P("docs", None),
    )
    return jax.shard_map(
        shards, mesh=mesh, in_specs=placed, out_specs=P("query", "docs", None), check_vma=False
    )
```

```python
import jax
import jax.numpy as jnp
from jax import lax
from jax.experimental import pallas as pl
from jax.experimental.pallas import tpu as pltpu
from jax.sharding import PartitionSpec as P

DOC_OWN = 8
R = 64
CAP = 4
DOCS = 64
TOK = 128
ROWS = DOCS * CAP
PANEL = 128
QUART = PANEL // 4
NT = (((1,), (1,)), ((), ()))


ACT_STEPS = (4096,)
GRAD_STEPS = (7168, 4096, 3072)


def project_kernel(act_hbm, grad_hbm, win_hbm, wout_hbm, len_hbm, own_hbm, panel_hbm,
                   rows_ref, quarter_ref, act_v, grad_v, win_v, wout_v, len_ref, own_ref, sems):
    jobs = []
    for x_hbm, w_hbm, x_v, w_v, sizes in (
        (act_hbm, win_hbm, act_v, win_v, ACT_STEPS),
        (grad_hbm, wout_hbm, grad_v, wout_v, GRAD_STEPS),
    ):
        at = 0
        for size in sizes:
            cols = pl.ds(at, size)
            n = 2 * len(jobs)
            copies = (
                pltpu.make_async_copy(w_hbm.at[:, cols], w_v.at[:, cols], sems.at[n]),
                pltpu.make_async_copy(x_hbm.at[0, :, cols], x_v.at[:, cols], sems.at[n + 1]),
            )
            for copy in copies:
                copy.start()
            jobs.append((copies, x_v, w_v, cols))
            at += size
    ints = (
        pltpu.make_async_copy(len_hbm, len_ref, sems.at[2 * len(jobs)]),
        pltpu.make_async_copy(own_hbm, own_ref, sems.at[2 * len(jobs) + 1]),
    )
    for copy in ints:
        copy.start()
    given = pl.multiple_of((quarter_of(lax.axis_index("docs")) ^ 1) * QUART, QUART)
    given = pltpu.make_async_copy(
        panel_hbm.at[pl.ds(given, QUART)], quarter_ref, sems.at[2 * len(jobs) + 2]
    )
    given.start()

    def low_part(job):
        copies, x_v, w_v, cols = job
        for copy in copies:
            copy.wait()
        return lax.dot_general(x_v[:, cols], w_v[:, cols], NT, preferred_element_type=jnp.float32)

    act_low = sum(low_part(job) for job in jobs[:len(ACT_STEPS)])

    for copy in ints:
        copy.wait()
    lens = len_ref[...].astype(jnp.float32)
    owners = own_ref[...].astype(jnp.float32)
    one = lax.broadcasted_iota(jnp.int32, (DOCS, DOCS), 0)
    other = lax.broadcasted_iota(jnp.int32, (DOCS, DOCS), 1)
    start = jnp.sum(jnp.where(other < one, lens, 0.0), axis=1, keepdims=True)
    size = jnp.sum(jnp.where(other == one, lens, 0.0), axis=1, keepdims=True)
    owner = jnp.sum(jnp.where(other == one, owners, 0.0), axis=1, keepdims=True)
    token = lax.broadcasted_iota(jnp.int32, (DOCS, TOK), 1).astype(jnp.float32)
    inside = (token >= start) & (token < start + size)
    goal = jnp.sum(jnp.where(inside, CAP * owner + token - start, 0.0), axis=0, keepdims=True)
    row = lax.broadcasted_iota(jnp.int32, (ROWS, TOK), 0).astype(jnp.float32)
    take = jnp.where(row == goal, 1.0, 0.0).astype(jnp.bfloat16)

    grad_low = sum(low_part(job) for job in jobs[len(ACT_STEPS):])
    rows = jnp.concatenate([grad_low, act_low], axis=1).astype(jnp.bfloat16)
    rows_ref[...] = jnp.dot(take, rows, preferred_element_type=jnp.float32).astype(jnp.bfloat16)
    given.wait()


def project(activations, out_grads, proj_in, proj_out, lengths, piece_owner, panels):
    width_in, width_out = activations.shape[-1], out_grads.shape[-1]
    hbm = pl.BlockSpec(memory_space=pltpu.HBM)
    vmem = pl.BlockSpec(memory_space=pltpu.VMEM)
    return pl.pallas_call(
        project_kernel,
        out_shape=(
            jax.ShapeDtypeStruct((ROWS, 2 * R), jnp.bfloat16),
            jax.ShapeDtypeStruct((QUART, panels.shape[1]), jnp.bfloat16),
        ),
        in_specs=[hbm] * 7,
        out_specs=(vmem, vmem),
        scratch_shapes=[
            pltpu.VMEM((TOK, width_in), jnp.bfloat16),
            pltpu.VMEM((TOK, width_out), jnp.bfloat16),
            pltpu.VMEM((R, width_in), jnp.bfloat16),
            pltpu.VMEM((R, width_out), jnp.bfloat16),
            pltpu.VMEM((1, DOCS), jnp.int32),
            pltpu.VMEM((1, DOCS), jnp.int32),
            pltpu.SemaphoreType.DMA((2 * len(ACT_STEPS + GRAD_STEPS) + 3,)),
        ],
        compiler_params=pltpu.CompilerParams(vmem_limit_bytes=56 << 20),
        cost_estimate=pl.CostEstimate(
            flops=2 * TOK * (width_in + width_out) * R,
            bytes_accessed=2 * (TOK + R) * (width_in + width_out),
            transcendentals=0,
        ),
        name="project",
    )(activations, out_grads, proj_in.T, proj_out.T, lengths, piece_owner, panels)


def call(kernel, out_shape, cost_us, in_specs, *given, **more):
    return pl.pallas_call(
        kernel,
        out_shape=out_shape,
        in_specs=in_specs,
        out_specs=pl.BlockSpec(memory_space=pltpu.VMEM),
        compiler_params=pltpu.CompilerParams(vmem_limit_bytes=16 << 20),
        cost_estimate=pl.CostEstimate(
            flops=cost_us * 10**9, bytes_accessed=cost_us * 10**6, transcendentals=0
        ),
        **more,
    )(*given)


def document_kernel(slot_ref, rows_ref, grads_ref):
    doc = lax.broadcasted_iota(jnp.int32, (DOC_OWN, DOCS), 0)
    mine = jnp.where(slot_ref[...] == doc, 1.0, 0.0).astype(jnp.bfloat16)
    source = lax.broadcasted_iota(jnp.int32, (DOCS, ROWS), 0)
    spread = jnp.where((lax.broadcasted_iota(jnp.int32, (DOCS, ROWS), 1) >> 2) == source, 1.0, 0.0)
    member = jnp.dot(mine, spread.astype(jnp.bfloat16), preferred_element_type=jnp.float32)

    rows = rows_ref[...]
    eye = (lax.broadcasted_iota(jnp.int32, (2 * R, 2 * R), 0)
           == lax.broadcasted_iota(jnp.int32, (2 * R, 2 * R), 1))
    eye = jnp.where(eye, 1.0, 0.0).astype(jnp.bfloat16)
    turned = lax.dot_general(eye, rows, NT, preferred_element_type=jnp.float32)
    masked = turned[:R][:, None, :] * member[None]
    masked = masked.reshape(R * DOC_OWN, ROWS).astype(jnp.bfloat16)
    wide = rows.astype(jnp.float32)
    lane = lax.broadcasted_iota(jnp.int32, (ROWS, 2 * R), 1)
    twice = jnp.where(lane < R, pltpu.roll(wide, R, 1), wide).astype(jnp.bfloat16)
    grads = jnp.dot(masked, twice, preferred_element_type=jnp.float32)
    grads = grads.reshape(R, DOC_OWN, 2 * R)
    low_half = lax.broadcasted_iota(jnp.int32, (DOC_OWN, 2 * R), 1) < R
    grads_ref[...] = jnp.concatenate(
        [jnp.where(low_half, grads[2 * i], grads[2 * i + 1]) for i in range(R // 2)], axis=1
    ).astype(jnp.bfloat16)


def against(panel_ref, grads):
    return lax.dot_general(panel_ref[...], grads, NT, preferred_element_type=jnp.float32)


def near_kernel(grads_ref, own_ref, beside_ref, out_ref):
    grads = grads_ref[...]
    out_ref[:, :PANEL] = jnp.transpose(against(own_ref, grads))
    out_ref[:, PANEL:] = jnp.transpose(against(beside_ref, grads))


def far_kernel(order_ref, grads_ref, near_ref, *refs):
    quarter_refs, out_ref, column_ref = refs[:-2], refs[-2], refs[-1]
    query_at = lax.axis_index("query")
    mine = quarter_of(lax.axis_index("docs"))
    grads = grads_ref[...]
    for n, ref in enumerate(quarter_refs):
        row = (n // 4) * PANEL + (mine ^ (n % 4)) * QUART
        column_ref[pl.ds(pl.multiple_of(row, QUART), QUART), :] = against(ref, grads)

    far = jnp.transpose(column_ref[...])
    blocks = [near_ref[:, :PANEL], near_ref[:, PANEL:], far[:, :PANEL], far[:, PANEL:]]
    for kth, block in enumerate(blocks):
        held = query_at ^ kth
        at = sum(jnp.where(order_ref[0, b] == held, b, 0) for b in range(1, 4)) * PANEL
        out_ref[0, :, pl.ds(pl.multiple_of(at, PANEL), PANEL)] = block


def quarter_of(docs_at):
    return (docs_at & 1) ^ (2 * ((docs_at >> 1) & 1)) ^ (3 * ((docs_at >> 3) & 1))


def hop(fn):
    pairs = []
    for z in range(8):
        for y in range(4):
            for x in range(4):
                for core in range(2):
                    at = []
                    for c in ((z, y, x, core), fn(z, y, x, core)):
                        at.append((((c[0] * 4 + c[1]) * 2 + c[2] % 2) * 2 + c[2] // 2) * 2 + c[3])
                    pairs.append(tuple(at))
    return pairs


TO_CORE = hop(lambda z, y, x, core: (z, y, x, 1 - core))
TO_CROSS = hop(lambda z, y, x, core: (z, y, 3 - x, core))
TO_X = hop(lambda z, y, x, core: (z, y, x ^ 1, core))
TO_Y = hop(lambda z, y, x, core: (z, y ^ 1, x, core))
TO_Z = hop(lambda z, y, x, core: (z ^ 1, y, x, core))


def send(value, pairs):
    return lax.ppermute(value, ("docs", "query"), pairs)


def shards(
    activations, out_grads, proj_in, proj_out, panels, lengths, piece_owner, doc_slot, panel_order
):
    smem = pl.BlockSpec(memory_space=pltpu.SMEM)
    vmem = pl.BlockSpec(memory_space=pltpu.VMEM)
    packed, given = project(
        activations, out_grads, proj_in, proj_out, lengths[0], piece_owner[0], panels
    )
    arrived = lax.all_to_all(
        packed.reshape(DOCS, CAP, 2 * R), "docs", split_axis=0, concat_axis=0, tiled=True
    ).reshape(ROWS, 2 * R)

    beside = send(panels, TO_CORE)
    across = send(given, TO_CROSS)
    parts = [across] + [send(across, to) for to in (TO_X, TO_Y, TO_Z)]
    parts_beside = [send(part, TO_CORE) for part in parts]

    grads = call(
        document_kernel, jax.ShapeDtypeStruct((DOC_OWN, R * R), jnp.bfloat16), 10,
        [vmem] * 2, doc_slot[0].reshape(1, DOCS), arrived, name="documents",
    )
    near = call(
        near_kernel, jax.ShapeDtypeStruct((DOC_OWN, 2 * PANEL), jnp.float32), 10,
        [vmem] * 3, grads, panels, beside, name="near",
    )
    return call(
        far_kernel, jax.ShapeDtypeStruct((1, DOC_OWN, 4 * PANEL), jnp.float32), 10,
        [smem] + [vmem] * 10, panel_order, grads, near, *parts, *parts_beside, name="far",
        scratch_shapes=[pltpu.VMEM((2 * PANEL, DOC_OWN), jnp.float32)],
    )


def solution(mesh):
    placed = (
        P("query", "docs", None),
        P("query", "docs", None),
        P(),
        P(),
        P("query", None),
        P("query", "docs", None),
        P("query", "docs", None),
        P("query", None, "docs"),
        P("docs", None),
    )
    return jax.shard_map(
        shards, mesh=mesh, in_specs=placed, out_specs=P("query", "docs", None), check_vma=False
    )
```

```python
import jax
import jax.numpy as jnp
from jax import lax
from jax.experimental import pallas as pl
from jax.experimental.pallas import tpu as pltpu
from jax.sharding import PartitionSpec as P

DOC_OWN = 8
R = 64
CAP = 4
DOCS = 64
TOK = 128
ROWS = DOCS * CAP
PANEL = 128
SHARE = 768
REST = R * R - 4 * SHARE
NT = (((1,), (1,)), ((), ()))
FIRST = 62


ACT_STEPS = (4096,)
GRAD_STEPS = (7168, 4096, 3072)


def project_kernel(act_hbm, grad_hbm, win_hbm, wout_hbm, len_hbm, own_hbm, panel_hbm,
                   rows_ref, share_ref, rest_ref, act_v, grad_v, win_v, wout_v, len_ref, own_ref, sems):
    jobs = []
    for x_hbm, w_hbm, x_v, w_v, sizes in (
        (act_hbm, win_hbm, act_v, win_v, ACT_STEPS),
        (grad_hbm, wout_hbm, grad_v, wout_v, GRAD_STEPS),
    ):
        at = 0
        for size in sizes:
            cols = pl.ds(at, size)
            n = 2 * len(jobs)
            copies = (
                pltpu.make_async_copy(w_hbm.at[:, cols], w_v.at[:, cols], sems.at[n]),
                pltpu.make_async_copy(x_hbm.at[0, :, cols], x_v.at[:, cols], sems.at[n + 1]),
            )
            for copy in copies:
                copy.start()
            jobs.append((copies, x_v, w_v, cols))
            at += size
    ints = (
        pltpu.make_async_copy(len_hbm, len_ref, sems.at[2 * len(jobs)]),
        pltpu.make_async_copy(own_hbm, own_ref, sems.at[2 * len(jobs) + 1]),
    )
    for copy in ints:
        copy.start()
    share = pl.multiple_of((share_of(lax.axis_index("docs")) ^ 1) * SHARE, SHARE)
    given = (
        pltpu.make_async_copy(
            panel_hbm.at[:, pl.ds(share, SHARE)], share_ref, sems.at[2 * len(jobs) + 2]
        ),
        pltpu.make_async_copy(
            panel_hbm.at[:, pl.ds(4 * SHARE, REST)], rest_ref, sems.at[2 * len(jobs) + 3]
        ),
    )
    for copy in given:
        copy.start()

    def low_part(job):
        copies, x_v, w_v, cols = job
        for copy in copies:
            copy.wait()
        return lax.dot_general(x_v[:, cols], w_v[:, cols], NT, preferred_element_type=jnp.float32)

    act_low = sum(low_part(job) for job in jobs[:len(ACT_STEPS)])

    for copy in ints:
        copy.wait()
    lens = len_ref[...].astype(jnp.float32)
    owners = (own_ref[...] ^ FIRST).astype(jnp.float32)
    one = lax.broadcasted_iota(jnp.int32, (DOCS, DOCS), 0)
    other = lax.broadcasted_iota(jnp.int32, (DOCS, DOCS), 1)
    start = jnp.sum(jnp.where(other < one, lens, 0.0), axis=1, keepdims=True)
    size = jnp.sum(jnp.where(other == one, lens, 0.0), axis=1, keepdims=True)
    owner = jnp.sum(jnp.where(other == one, owners, 0.0), axis=1, keepdims=True)
    token = lax.broadcasted_iota(jnp.int32, (DOCS, TOK), 1).astype(jnp.float32)
    inside = (token >= start) & (token < start + size)
    goal = jnp.sum(jnp.where(inside, CAP * owner + token - start, 0.0), axis=0, keepdims=True)
    row = lax.broadcasted_iota(jnp.int32, (ROWS, TOK), 0).astype(jnp.float32)
    take = jnp.where(row == goal, 1.0, 0.0).astype(jnp.bfloat16)

    grad_low = sum(low_part(job) for job in jobs[len(ACT_STEPS):])
    rows = jnp.concatenate([grad_low, act_low], axis=1).astype(jnp.bfloat16)
    rows_ref[...] = jnp.dot(take, rows, preferred_element_type=jnp.float32).astype(jnp.bfloat16)
    for copy in given:
        copy.wait()


def project(activations, out_grads, proj_in, proj_out, lengths, piece_owner, panels):
    width_in, width_out = activations.shape[-1], out_grads.shape[-1]
    hbm = pl.BlockSpec(memory_space=pltpu.HBM)
    vmem = pl.BlockSpec(memory_space=pltpu.VMEM)
    return pl.pallas_call(
        project_kernel,
        out_shape=(
            jax.ShapeDtypeStruct((ROWS, 2 * R), jnp.bfloat16),
            jax.ShapeDtypeStruct((PANEL, SHARE), jnp.bfloat16),
            jax.ShapeDtypeStruct((PANEL, REST), jnp.bfloat16),
        ),
        in_specs=[hbm] * 7,
        out_specs=(vmem, vmem, vmem),
        scratch_shapes=[
            pltpu.VMEM((TOK, width_in), jnp.bfloat16),
            pltpu.VMEM((TOK, width_out), jnp.bfloat16),
            pltpu.VMEM((R, width_in), jnp.bfloat16),
            pltpu.VMEM((R, width_out), jnp.bfloat16),
            pltpu.VMEM((1, DOCS), jnp.int32),
            pltpu.VMEM((1, DOCS), jnp.int32),
            pltpu.SemaphoreType.DMA((2 * len(ACT_STEPS + GRAD_STEPS) + 4,)),
        ],
        compiler_params=pltpu.CompilerParams(vmem_limit_bytes=56 << 20),
        cost_estimate=pl.CostEstimate(
            flops=2 * TOK * (width_in + width_out) * R,
            bytes_accessed=2 * (TOK + R) * (width_in + width_out),
            transcendentals=0,
        ),
        name="project",
    )(activations, out_grads, proj_in.T, proj_out.T, lengths, piece_owner, panels)


def call(kernel, out_shape, cost_us, in_specs, *given, **more):
    return pl.pallas_call(
        kernel,
        out_shape=out_shape,
        in_specs=in_specs,
        out_specs=jax.tree.map(lambda _: pl.BlockSpec(memory_space=pltpu.VMEM), out_shape),
        compiler_params=pltpu.CompilerParams(vmem_limit_bytes=16 << 20),
        cost_estimate=pl.CostEstimate(
            flops=cost_us * 10**9, bytes_accessed=cost_us * 10**6, transcendentals=0
        ),
        **more,
    )(*given)


def document_kernel(slot_ref, rows_ref, grads_ref):
    doc = lax.broadcasted_iota(jnp.int32, (DOC_OWN, DOCS), 0)
    mine = jnp.where(slot_ref[...] == doc, 1.0, 0.0).astype(jnp.bfloat16)
    source = lax.broadcasted_iota(jnp.int32, (DOCS, ROWS), 0)
    place = lax.broadcasted_iota(jnp.int32, (DOCS, ROWS), 1) >> 2
    spread = jnp.where((place ^ FIRST) == source, 1.0, 0.0)
    member = jnp.dot(mine, spread.astype(jnp.bfloat16), preferred_element_type=jnp.float32)

    rows = rows_ref[...]
    eye = (lax.broadcasted_iota(jnp.int32, (2 * R, 2 * R), 0)
           == lax.broadcasted_iota(jnp.int32, (2 * R, 2 * R), 1))
    eye = jnp.where(eye, 1.0, 0.0).astype(jnp.bfloat16)
    turned = lax.dot_general(eye, rows, NT, preferred_element_type=jnp.float32)
    masked = turned[:R][:, None, :] * member[None]
    masked = masked.reshape(R * DOC_OWN, ROWS).astype(jnp.bfloat16)
    wide = rows.astype(jnp.float32)
    lane = lax.broadcasted_iota(jnp.int32, (ROWS, 2 * R), 1)
    twice = jnp.where(lane < R, pltpu.roll(wide, R, 1), wide).astype(jnp.bfloat16)
    grads = jnp.dot(masked, twice, preferred_element_type=jnp.float32)
    grads = grads.reshape(R, DOC_OWN, 2 * R)
    low_half = lax.broadcasted_iota(jnp.int32, (DOC_OWN, 2 * R), 1) < R
    grads_ref[...] = jnp.concatenate(
        [jnp.where(low_half, grads[2 * i], grads[2 * i + 1]) for i in range(R // 2)], axis=1
    ).astype(jnp.bfloat16)


def against(grads_ref, panel_ref, at):
    grads = grads_ref[:, pl.ds(at, panel_ref.shape[1])]
    return lax.dot_general(grads, panel_ref[...], NT, preferred_element_type=jnp.float32)


def share_at(kth):
    return pl.multiple_of((share_of(lax.axis_index("docs")) ^ kth) * SHARE, SHARE)


def near_kernel(grads_ref, own_ref, across_ref, out_ref):
    out_ref[:, :PANEL] = against(grads_ref, own_ref, 0)
    out_ref[:, PANEL:] = against(grads_ref, across_ref, share_at(0))


def far_kernel(grads_ref, mate_grads_ref, near_ref, mate_near_ref, rest_ref, *refs):
    part_refs, out_ref, mate_out_ref = refs[:-2], refs[-2], refs[-1]
    both = None
    for ref, at in [(rest_ref, 4 * SHARE)] + [(r, share_at(k + 1)) for k, r in enumerate(part_refs)]:
        cols = pl.ds(at, ref.shape[1])
        grads = jnp.concatenate([grads_ref[:, cols], mate_grads_ref[:, cols]], axis=0)
        part = lax.dot_general(grads, ref[...], NT, preferred_element_type=jnp.float32)
        both = part if both is None else both + part
    out_ref[...] = near_ref[:, PANEL:] + both[:DOC_OWN]
    mate_out_ref[:, :PANEL] = mate_near_ref[:, :PANEL]
    mate_out_ref[:, PANEL:] = mate_near_ref[:, PANEL:] + both[DOC_OWN:]


def last_kernel(order_ref, near_ref, far_ref, mate_ref, out_ref):
    query_at = lax.axis_index("query")

    def put(kth, block):
        held = query_at ^ kth
        at = sum(jnp.where(order_ref[0, b] == held, b, 0) for b in range(1, 4)) * PANEL
        out_ref[0, :, pl.ds(pl.multiple_of(at, PANEL), PANEL)] = block

    put(0, near_ref[:, :PANEL])
    put(1, mate_ref[:, :PANEL])
    put(2, far_ref[...])
    put(3, mate_ref[:, PANEL:])


def share_of(docs_at):
    return (docs_at & 1) ^ (2 * ((docs_at >> 1) & 1)) ^ (3 * ((docs_at >> 3) & 1))


def hop(fn):
    pairs = []
    for z in range(8):
        for y in range(4):
            for x in range(4):
                for core in range(2):
                    at = []
                    for c in ((z, y, x, core), fn(z, y, x, core)):
                        at.append((((c[0] * 4 + c[1]) * 2 + c[2] % 2) * 2 + c[2] // 2) * 2 + c[3])
                    pairs.append(tuple(at))
    return pairs


TO_CORE = hop(lambda z, y, x, core: (z, y, x, 1 - core))
TO_CROSS = hop(lambda z, y, x, core: (z, y, 3 - x, core))
TO_X = hop(lambda z, y, x, core: (z, y, x ^ 1, core))
TO_Y = hop(lambda z, y, x, core: (z, y ^ 1, x, core))
TO_Z = hop(lambda z, y, x, core: (z ^ 1, y, x, core))


def send(value, pairs):
    return lax.ppermute(value, ("docs", "query"), pairs)


def shards(
    activations, out_grads, proj_in, proj_out, panels, lengths, piece_owner, doc_slot, panel_order
):
    smem = pl.BlockSpec(memory_space=pltpu.SMEM)
    vmem = pl.BlockSpec(memory_space=pltpu.VMEM)
    packed, share, rest = project(
        activations, out_grads, proj_in, proj_out, lengths[0], piece_owner[0], panels
    )
    arrived = lax.all_to_all(
        packed.reshape(DOCS, CAP, 2 * R), "docs", split_axis=0, concat_axis=0, tiled=True,
        axis_index_groups=[[place ^ FIRST for place in range(DOCS)]],
    ).reshape(ROWS, 2 * R)

    across = send(share, TO_CROSS)
    rest = send(rest, TO_CROSS)
    parts = [send(across, to) for to in (TO_X, TO_Y, TO_Z)]

    def block(width):
        return jax.ShapeDtypeStruct((DOC_OWN, width), jnp.float32)

    grads = call(
        document_kernel, jax.ShapeDtypeStruct((DOC_OWN, R * R), jnp.bfloat16), 10,
        [vmem] * 2, doc_slot[0].reshape(1, DOCS), arrived, name="documents",
    )
    mate_grads = send(grads, TO_CORE)
    near = call(
        near_kernel, block(2 * PANEL), 0, [vmem] * 3, grads, panels, across, name="near",
    )
    near, mate_grads = lax.optimization_barrier((near, mate_grads))
    mate_near = call(
        near_kernel, block(2 * PANEL), 0, [vmem] * 3, mate_grads, panels, across, name="mate",
    )
    far, mate_scores = call(
        far_kernel, (block(PANEL), block(2 * PANEL)), 0, [vmem] * 8,
        grads, mate_grads, near, mate_near, rest, *parts, name="far",
    )
    mate_scores = send(mate_scores, TO_CORE)
    return call(
        last_kernel, jax.ShapeDtypeStruct((1, DOC_OWN, 4 * PANEL), jnp.float32), 0,
        [smem] + [vmem] * 3, panel_order, near, far, mate_scores, name="last",
    )


def solution(mesh):
    placed = (
        P("query", "docs", None),
        P("query", "docs", None),
        P(),
        P(),
        P("query", None),
        P("query", "docs", None),
        P("query", "docs", None),
        P("query", None, "docs"),
        P("docs", None),
    )
    return jax.shard_map(
        shards, mesh=mesh, in_specs=placed, out_specs=P("query", "docs", None), check_vma=False
    )
```

```python
import jax
import jax.numpy as jnp
from jax import lax
from jax.experimental import pallas as pl
from jax.experimental.pallas import tpu as pltpu
from jax.sharding import PartitionSpec as P

DOC_OWN = 8
R = 64
CAP = 4
DOCS = 64
TOK = 128
ROWS = DOCS * CAP
PANEL = 128
SHARE = 768
REST = R * R - 4 * SHARE
NT = (((1,), (1,)), ((), ()))
FIRST = 62


ACT_STEPS = (4096,)
GRAD_STEPS = (7168, 4096, 3072)


def project_kernel(act_hbm, grad_hbm, win_hbm, wout_hbm, len_hbm, own_hbm, panel_hbm,
                   rows_ref, share_ref, rest_ref, act_v, grad_v, win_v, wout_v, len_ref, own_ref, sems):
    jobs = []
    for x_hbm, w_hbm, x_v, w_v, sizes in (
        (act_hbm, win_hbm, act_v, win_v, ACT_STEPS),
        (grad_hbm, wout_hbm, grad_v, wout_v, GRAD_STEPS),
    ):
        at = 0
        for size in sizes:
            cols = pl.ds(at, size)
            n = 2 * len(jobs)
            copies = (
                pltpu.make_async_copy(w_hbm.at[:, cols], w_v.at[:, cols], sems.at[n]),
                pltpu.make_async_copy(x_hbm.at[0, :, cols], x_v.at[:, cols], sems.at[n + 1]),
            )
            for copy in copies:
                copy.start()
            jobs.append((copies, x_v, w_v, cols))
            at += size
    ints = (
        pltpu.make_async_copy(len_hbm, len_ref, sems.at[2 * len(jobs)]),
        pltpu.make_async_copy(own_hbm, own_ref, sems.at[2 * len(jobs) + 1]),
    )
    for copy in ints:
        copy.start()
    share = pl.multiple_of((share_of(lax.axis_index("docs")) ^ 1) * SHARE, SHARE)
    given = (
        pltpu.make_async_copy(
            panel_hbm.at[:, pl.ds(share, SHARE)], share_ref, sems.at[2 * len(jobs) + 2]
        ),
        pltpu.make_async_copy(
            panel_hbm.at[:, pl.ds(4 * SHARE, REST)], rest_ref, sems.at[2 * len(jobs) + 3]
        ),
    )
    for copy in given:
        copy.start()

    def low_part(job):
        copies, x_v, w_v, cols = job
        for copy in copies:
            copy.wait()
        return lax.dot_general(x_v[:, cols], w_v[:, cols], NT, preferred_element_type=jnp.float32)

    act_low = sum(low_part(job) for job in jobs[:len(ACT_STEPS)])

    for copy in ints:
        copy.wait()
    lens = len_ref[...].astype(jnp.float32)
    owners = (own_ref[...] ^ FIRST).astype(jnp.float32)
    one = lax.broadcasted_iota(jnp.int32, (DOCS, DOCS), 0)
    other = lax.broadcasted_iota(jnp.int32, (DOCS, DOCS), 1)
    start = jnp.sum(jnp.where(other < one, lens, 0.0), axis=1, keepdims=True)
    size = jnp.sum(jnp.where(other == one, lens, 0.0), axis=1, keepdims=True)
    owner = jnp.sum(jnp.where(other == one, owners, 0.0), axis=1, keepdims=True)
    token = lax.broadcasted_iota(jnp.int32, (DOCS, TOK), 1).astype(jnp.float32)
    inside = (token >= start) & (token < start + size)
    goal = jnp.sum(jnp.where(inside, CAP * owner + token - start, 0.0), axis=0, keepdims=True)
    row = lax.broadcasted_iota(jnp.int32, (ROWS, TOK), 0).astype(jnp.float32)
    take = jnp.where(row == goal, 1.0, 0.0).astype(jnp.bfloat16)

    grad_low = sum(low_part(job) for job in jobs[len(ACT_STEPS):])
    rows = jnp.concatenate([grad_low, act_low], axis=1).astype(jnp.bfloat16)
    rows_ref[...] = jnp.dot(take, rows, preferred_element_type=jnp.float32).astype(jnp.bfloat16)
    for copy in given:
        copy.wait()


def project(activations, out_grads, proj_in, proj_out, lengths, piece_owner, panels):
    width_in, width_out = activations.shape[-1], out_grads.shape[-1]
    hbm = pl.BlockSpec(memory_space=pltpu.HBM)
    vmem = pl.BlockSpec(memory_space=pltpu.VMEM)
    return pl.pallas_call(
        project_kernel,
        out_shape=(
            jax.ShapeDtypeStruct((ROWS, 2 * R), jnp.bfloat16),
            jax.ShapeDtypeStruct((PANEL, SHARE), jnp.bfloat16),
            jax.ShapeDtypeStruct((PANEL, REST), jnp.bfloat16),
        ),
        in_specs=[hbm] * 7,
        out_specs=(vmem, vmem, vmem),
        scratch_shapes=[
            pltpu.VMEM((TOK, width_in), jnp.bfloat16),
            pltpu.VMEM((TOK, width_out), jnp.bfloat16),
            pltpu.VMEM((R, width_in), jnp.bfloat16),
            pltpu.VMEM((R, width_out), jnp.bfloat16),
            pltpu.VMEM((1, DOCS), jnp.int32),
            pltpu.VMEM((1, DOCS), jnp.int32),
            pltpu.SemaphoreType.DMA((2 * len(ACT_STEPS + GRAD_STEPS) + 4,)),
        ],
        compiler_params=pltpu.CompilerParams(vmem_limit_bytes=56 << 20),
        cost_estimate=pl.CostEstimate(
            flops=2 * TOK * (width_in + width_out) * R,
            bytes_accessed=2 * (TOK + R) * (width_in + width_out),
            transcendentals=0,
        ),
        name="project",
    )(activations, out_grads, proj_in.T, proj_out.T, lengths, piece_owner, panels)


def call(kernel, out_shape, cost_us, in_specs, *given, **more):
    return pl.pallas_call(
        kernel,
        out_shape=out_shape,
        in_specs=in_specs,
        out_specs=jax.tree.map(lambda _: pl.BlockSpec(memory_space=pltpu.VMEM), out_shape),
        compiler_params=pltpu.CompilerParams(vmem_limit_bytes=16 << 20),
        cost_estimate=pl.CostEstimate(
            flops=cost_us * 10**9, bytes_accessed=cost_us * 10**6, transcendentals=0
        ),
        **more,
    )(*given)


def document_kernel(slot_ref, rows_ref, panel_ref, grads_ref):
    doc = lax.broadcasted_iota(jnp.int32, (DOC_OWN, DOCS), 0)
    mine = jnp.where(slot_ref[...] == doc, 1.0, 0.0).astype(jnp.bfloat16)
    source = lax.broadcasted_iota(jnp.int32, (DOCS, ROWS), 0)
    place = lax.broadcasted_iota(jnp.int32, (DOCS, ROWS), 1) >> 2
    spread = jnp.where((place ^ FIRST) == source, 1.0, 0.0)
    member = jnp.dot(mine, spread.astype(jnp.bfloat16), preferred_element_type=jnp.float32)

    rows = rows_ref[...]
    eye = (lax.broadcasted_iota(jnp.int32, (2 * R, 2 * R), 0)
           == lax.broadcasted_iota(jnp.int32, (2 * R, 2 * R), 1))
    eye = jnp.where(eye, 1.0, 0.0).astype(jnp.bfloat16)
    turned = lax.dot_general(eye, rows, NT, preferred_element_type=jnp.float32)
    masked = turned[:R][:, None, :] * member[None]
    masked = masked.reshape(R * DOC_OWN, ROWS).astype(jnp.bfloat16)
    wide = rows.astype(jnp.float32)
    lane = lax.broadcasted_iota(jnp.int32, (ROWS, 2 * R), 1)
    twice = jnp.where(lane < R, pltpu.roll(wide, R, 1), wide).astype(jnp.bfloat16)
    grads = jnp.dot(masked, twice, preferred_element_type=jnp.float32)
    grads = grads.reshape(R, DOC_OWN, 2 * R)
    low_half = lax.broadcasted_iota(jnp.int32, (DOC_OWN, 2 * R), 1) < R
    grads_ref[...] = jnp.concatenate(
        [jnp.where(low_half, grads[2 * i], grads[2 * i + 1]) for i in range(R // 2)], axis=1
    ).astype(jnp.bfloat16)


def against(grads_ref, panel_ref, at):
    grads = grads_ref[:, pl.ds(at, panel_ref.shape[1])]
    return lax.dot_general(grads, panel_ref[...], NT, preferred_element_type=jnp.float32)


def share_at(kth):
    return pl.multiple_of((share_of(lax.axis_index("docs")) ^ kth) * SHARE, SHARE)


def near_kernel(grads_ref, own_ref, across_ref, out_ref):
    out_ref[:, :PANEL] = against(grads_ref, own_ref, 0)
    out_ref[:, PANEL:] = against(grads_ref, across_ref, share_at(0))


def far_kernel(grads_ref, mate_grads_ref, near_ref, mate_near_ref, rest_ref, *refs):
    part_refs, out_ref, mate_out_ref = refs[:-2], refs[-2], refs[-1]
    both = None
    for ref, at in [(rest_ref, 4 * SHARE)] + [(r, share_at(k + 1)) for k, r in enumerate(part_refs)]:
        cols = pl.ds(at, ref.shape[1])
        grads = jnp.concatenate([grads_ref[:, cols], mate_grads_ref[:, cols]], axis=0)
        part = lax.dot_general(grads, ref[...], NT, preferred_element_type=jnp.float32)
        both = part if both is None else both + part
    out_ref[...] = near_ref[:, PANEL:] + both[:DOC_OWN]
    mate_out_ref[:, :PANEL] = mate_near_ref[:, :PANEL]
    mate_out_ref[:, PANEL:] = mate_near_ref[:, PANEL:] + both[DOC_OWN:]


def last_kernel(order_ref, near_ref, far_ref, mate_ref, out_ref):
    query_at = lax.axis_index("query")

    blocks = [near_ref[:, :PANEL], mate_ref[:, :PANEL], far_ref[...], mate_ref[:, PANEL:]]
    for at in range(4):
        wanted = order_ref[:, at:at + 1]
        out_ref[0, :, at * PANEL:(at + 1) * PANEL] = sum(
            jnp.where(wanted == (query_at ^ kth), block, 0.0) for kth, block in enumerate(blocks)
        )


def share_of(docs_at):
    return (docs_at & 1) ^ (2 * ((docs_at >> 1) & 1)) ^ (3 * ((docs_at >> 3) & 1))


def hop(fn):
    pairs = []
    for z in range(8):
        for y in range(4):
            for x in range(4):
                for core in range(2):
                    at = []
                    for c in ((z, y, x, core), fn(z, y, x, core)):
                        at.append((((c[0] * 4 + c[1]) * 2 + c[2] % 2) * 2 + c[2] // 2) * 2 + c[3])
                    pairs.append(tuple(at))
    return pairs


TO_CORE = hop(lambda z, y, x, core: (z, y, x, 1 - core))
TO_CROSS = hop(lambda z, y, x, core: (z, y, 3 - x, core))
TO_X = hop(lambda z, y, x, core: (z, y, x ^ 1, core))
TO_Y = hop(lambda z, y, x, core: (z, y ^ 1, x, core))
TO_Z = hop(lambda z, y, x, core: (z ^ 1, y, x, core))


def send(value, pairs):
    return lax.ppermute(value, ("docs", "query"), pairs)


def shards(
    activations, out_grads, proj_in, proj_out, panels, lengths, piece_owner, doc_slot, panel_order
):
    vmem = pl.BlockSpec(memory_space=pltpu.VMEM)
    packed, share, rest = project(
        activations, out_grads, proj_in, proj_out, lengths[0], piece_owner[0], panels
    )
    arrived = lax.all_to_all(
        packed.reshape(DOCS, CAP, 2 * R), "docs", split_axis=0, concat_axis=0, tiled=True,
        axis_index_groups=[[place ^ FIRST for place in range(DOCS)]],
    ).reshape(ROWS, 2 * R)

    across = send(share, TO_CROSS)
    rest = send(rest, TO_CROSS)
    parts = [send(across, to) for to in (TO_X, TO_Y, TO_Z)]

    def block(width):
        return jax.ShapeDtypeStruct((DOC_OWN, width), jnp.float32)

    grads = call(
        document_kernel, jax.ShapeDtypeStruct((DOC_OWN, R * R), jnp.bfloat16), 10,
        [vmem] * 3, doc_slot[0].reshape(1, DOCS), arrived, panels, name="documents",
    )
    mate_grads = send(grads, TO_CORE)
    near = call(
        near_kernel, block(2 * PANEL), 0, [vmem] * 3, grads, panels, across, name="near",
    )
    near, mate_grads = lax.optimization_barrier((near, mate_grads))
    mate_near = call(
        near_kernel, block(2 * PANEL), 0, [vmem] * 3, mate_grads, panels, across, name="mate",
    )
    far, mate_scores = call(
        far_kernel, (block(PANEL), block(2 * PANEL)), 0, [vmem] * 8,
        grads, mate_grads, near, mate_near, rest, *parts, name="far",
    )
    mate_scores = send(mate_scores, TO_CORE)
    return call(
        last_kernel, jax.ShapeDtypeStruct((1, DOC_OWN, 4 * PANEL), jnp.float32), 0,
        [vmem] * 4, panel_order, near, far, mate_scores, name="last",
    )


def solution(mesh):
    placed = (
        P("query", "docs", None),
        P("query", "docs", None),
        P(),
        P(),
        P("query", None),
        P("query", "docs", None),
        P("query", "docs", None),
        P("query", None, "docs"),
        P("docs", None),
    )
    return jax.shard_map(
        shards, mesh=mesh, in_specs=placed, out_specs=P("query", "docs", None), check_vma=False
    )
```

```python
import jax
import jax.numpy as jnp
from jax import lax
from jax.experimental import pallas as pl
from jax.experimental.pallas import tpu as pltpu
from jax.sharding import PartitionSpec as P

DOC_OWN = 8
R = 64
CAP = 4
DOCS = 64
TOK = 128
ROWS = DOCS * CAP
PANEL = 128
SHARE = 768
REST = R * R - 4 * SHARE
NT = (((1,), (1,)), ((), ()))
FIRST = 62


ACT_STEPS = (4096,)
GRAD_STEPS = (7168, 4096, 3072)


GIVEN_US = 10


def given_kernel(panel_hbm, share_ref, rest_ref, sems):
    share = pl.multiple_of((share_of(lax.axis_index("docs")) ^ 1) * SHARE, SHARE)
    copies = (
        pltpu.make_async_copy(panel_hbm.at[:, pl.ds(share, SHARE)], share_ref, sems.at[0]),
        pltpu.make_async_copy(panel_hbm.at[:, pl.ds(4 * SHARE, REST)], rest_ref, sems.at[1]),
    )
    for copy in copies:
        copy.start()
    for copy in copies:
        copy.wait()


def given(panels):
    return pl.pallas_call(
        given_kernel,
        out_shape=(
            jax.ShapeDtypeStruct((PANEL, SHARE), jnp.bfloat16),
            jax.ShapeDtypeStruct((PANEL, REST), jnp.bfloat16),
        ),
        in_specs=[pl.BlockSpec(memory_space=pltpu.HBM)],
        out_specs=(pl.BlockSpec(memory_space=pltpu.VMEM),) * 2,
        scratch_shapes=[pltpu.SemaphoreType.DMA((2,))],
        compiler_params=pltpu.CompilerParams(vmem_limit_bytes=8 << 20),
        cost_estimate=pl.CostEstimate(flops=GIVEN_US * 10**9, bytes_accessed=GIVEN_US * 10**6, transcendentals=0),
        name="given",
    )(panels)


def take_kernel(len_ref, own_ref, take_ref):
    lens = len_ref[...].astype(jnp.float32)
    owners = (own_ref[...] ^ FIRST).astype(jnp.float32)
    one = lax.broadcasted_iota(jnp.int32, (DOCS, DOCS), 0)
    other = lax.broadcasted_iota(jnp.int32, (DOCS, DOCS), 1)
    start = jnp.sum(jnp.where(other < one, lens, 0.0), axis=1, keepdims=True)
    size = jnp.sum(jnp.where(other == one, lens, 0.0), axis=1, keepdims=True)
    owner = jnp.sum(jnp.where(other == one, owners, 0.0), axis=1, keepdims=True)
    token = lax.broadcasted_iota(jnp.int32, (DOCS, TOK), 1).astype(jnp.float32)
    inside = (token >= start) & (token < start + size)
    goal = jnp.sum(jnp.where(inside, CAP * owner + token - start, 0.0), axis=0, keepdims=True)
    row = lax.broadcasted_iota(jnp.int32, (ROWS, TOK), 0).astype(jnp.float32)
    take_ref[...] = jnp.where(row == goal, 1.0, 0.0).astype(jnp.bfloat16)


def grad_kernel(grad_ref, wout_ref, low_ref):
    low_ref[...] = lax.dot_general(grad_ref[0], wout_ref[...], NT, preferred_element_type=jnp.float32)


def pack_kernel(act_ref, win_ref, take_ref, low_ref, rows_ref):
    act_low = lax.dot_general(act_ref[0], win_ref[...], NT, preferred_element_type=jnp.float32)
    rows = jnp.concatenate([low_ref[...], act_low], axis=1).astype(jnp.bfloat16)
    rows_ref[...] = jnp.dot(
        take_ref[...], rows, preferred_element_type=jnp.float32
    ).astype(jnp.bfloat16)


def project(activations, out_grads, proj_in, proj_out, lengths, piece_owner):
    vmem = pl.BlockSpec(memory_space=pltpu.VMEM)
    take = call(
        take_kernel, jax.ShapeDtypeStruct((ROWS, TOK), jnp.bfloat16), 0, [vmem] * 2,
        lengths, piece_owner, name="take",
    )
    grad_low = call(
        grad_kernel, jax.ShapeDtypeStruct((TOK, R), jnp.float32), 0, [vmem] * 2,
        out_grads, proj_out.T, name="grads",
    )
    return call(
        pack_kernel, jax.ShapeDtypeStruct((ROWS, 2 * R), jnp.bfloat16), 10, [vmem] * 4,
        activations, proj_in.T, take, grad_low, name="pack",
    )


def call(kernel, out_shape, cost_us, in_specs, *given, **more):
    return pl.pallas_call(
        kernel,
        out_shape=out_shape,
        in_specs=in_specs,
        out_specs=jax.tree.map(lambda _: pl.BlockSpec(memory_space=pltpu.VMEM), out_shape),
        compiler_params=pltpu.CompilerParams(vmem_limit_bytes=16 << 20),
        cost_estimate=pl.CostEstimate(
            flops=cost_us * 10**9, bytes_accessed=cost_us * 10**6, transcendentals=0
        ),
        **more,
    )(*given)


def document_kernel(slot_ref, rows_ref, panel_ref, grads_ref):
    doc = lax.broadcasted_iota(jnp.int32, (DOC_OWN, DOCS), 0)
    mine = jnp.where(slot_ref[...] == doc, 1.0, 0.0).astype(jnp.bfloat16)
    source = lax.broadcasted_iota(jnp.int32, (DOCS, ROWS), 0)
    place = lax.broadcasted_iota(jnp.int32, (DOCS, ROWS), 1) >> 2
    spread = jnp.where((place ^ FIRST) == source, 1.0, 0.0)
    member = jnp.dot(mine, spread.astype(jnp.bfloat16), preferred_element_type=jnp.float32)

    rows = rows_ref[...]
    eye = (lax.broadcasted_iota(jnp.int32, (2 * R, 2 * R), 0)
           == lax.broadcasted_iota(jnp.int32, (2 * R, 2 * R), 1))
    eye = jnp.where(eye, 1.0, 0.0).astype(jnp.bfloat16)
    turned = lax.dot_general(eye, rows, NT, preferred_element_type=jnp.float32)
    masked = turned[:R][:, None, :] * member[None]
    masked = masked.reshape(R * DOC_OWN, ROWS).astype(jnp.bfloat16)
    wide = rows.astype(jnp.float32)
    lane = lax.broadcasted_iota(jnp.int32, (ROWS, 2 * R), 1)
    twice = jnp.where(lane < R, pltpu.roll(wide, R, 1), wide).astype(jnp.bfloat16)
    grads = jnp.dot(masked, twice, preferred_element_type=jnp.float32)
    grads = grads.reshape(R, DOC_OWN, 2 * R)
    low_half = lax.broadcasted_iota(jnp.int32, (DOC_OWN, 2 * R), 1) < R
    grads_ref[...] = jnp.concatenate(
        [jnp.where(low_half, grads[2 * i], grads[2 * i + 1]) for i in range(R // 2)], axis=1
    ).astype(jnp.bfloat16)


def against(grads_ref, panel_ref, at):
    grads = grads_ref[:, pl.ds(at, panel_ref.shape[1])]
    return lax.dot_general(grads, panel_ref[...], NT, preferred_element_type=jnp.float32)


def share_at(kth):
    return pl.multiple_of((share_of(lax.axis_index("docs")) ^ kth) * SHARE, SHARE)


def near_kernel(grads_ref, own_ref, across_ref, out_ref):
    out_ref[:, :PANEL] = against(grads_ref, own_ref, 0)
    out_ref[:, PANEL:] = against(grads_ref, across_ref, share_at(0))


def far_kernel(grads_ref, mate_grads_ref, near_ref, mate_near_ref, rest_ref, *refs):
    part_refs, out_ref, mate_out_ref = refs[:-2], refs[-2], refs[-1]
    both = None
    for ref, at in [(rest_ref, 4 * SHARE)] + [(r, share_at(k + 1)) for k, r in enumerate(part_refs)]:
        cols = pl.ds(at, ref.shape[1])
        grads = jnp.concatenate([grads_ref[:, cols], mate_grads_ref[:, cols]], axis=0)
        part = lax.dot_general(grads, ref[...], NT, preferred_element_type=jnp.float32)
        both = part if both is None else both + part
    out_ref[...] = near_ref[:, PANEL:] + both[:DOC_OWN]
    mate_out_ref[:, :PANEL] = mate_near_ref[:, :PANEL]
    mate_out_ref[:, PANEL:] = mate_near_ref[:, PANEL:] + both[DOC_OWN:]


def last_kernel(order_ref, near_ref, far_ref, mate_ref, out_ref):
    query_at = lax.axis_index("query")

    blocks = [near_ref[:, :PANEL], mate_ref[:, :PANEL], far_ref[...], mate_ref[:, PANEL:]]
    for at in range(4):
        wanted = order_ref[:, at:at + 1]
        out_ref[0, :, at * PANEL:(at + 1) * PANEL] = sum(
            jnp.where(wanted == (query_at ^ kth), block, 0.0) for kth, block in enumerate(blocks)
        )


def share_of(docs_at):
    return (docs_at & 1) ^ (2 * ((docs_at >> 1) & 1)) ^ (3 * ((docs_at >> 3) & 1))


def hop(fn):
    pairs = []
    for z in range(8):
        for y in range(4):
            for x in range(4):
                for core in range(2):
                    at = []
                    for c in ((z, y, x, core), fn(z, y, x, core)):
                        at.append((((c[0] * 4 + c[1]) * 2 + c[2] % 2) * 2 + c[2] // 2) * 2 + c[3])
                    pairs.append(tuple(at))
    return pairs


TO_CORE = hop(lambda z, y, x, core: (z, y, x, 1 - core))
TO_CROSS = hop(lambda z, y, x, core: (z, y, 3 - x, core))
TO_X = hop(lambda z, y, x, core: (z, y, x ^ 1, core))
TO_Y = hop(lambda z, y, x, core: (z, y ^ 1, x, core))
TO_Z = hop(lambda z, y, x, core: (z ^ 1, y, x, core))


def send(value, pairs):
    return lax.ppermute(value, ("docs", "query"), pairs)


def shards(
    activations, out_grads, proj_in, proj_out, panels, lengths, piece_owner, doc_slot, panel_order
):
    vmem = pl.BlockSpec(memory_space=pltpu.VMEM)
    share, rest = given(panels)
    packed = project(activations, out_grads, proj_in, proj_out, lengths[0], piece_owner[0])
    arrived = lax.all_to_all(
        packed.reshape(DOCS, CAP, 2 * R), "docs", split_axis=0, concat_axis=0, tiled=True,
        axis_index_groups=[[place ^ FIRST for place in range(DOCS)]],
    ).reshape(ROWS, 2 * R)

    across = send(share, TO_CROSS)
    rest = send(rest, TO_CROSS)
    parts = [send(across, to) for to in (TO_X, TO_Y, TO_Z)]

    def block(width):
        return jax.ShapeDtypeStruct((DOC_OWN, width), jnp.float32)

    grads = call(
        document_kernel, jax.ShapeDtypeStruct((DOC_OWN, R * R), jnp.bfloat16), 10,
        [vmem] * 3, doc_slot[0].reshape(1, DOCS), arrived, panels, name="documents",
    )
    mate_grads = send(grads, TO_CORE)
    near = call(
        near_kernel, block(2 * PANEL), 0, [vmem] * 3, grads, panels, across, name="near",
    )
    near, mate_grads = lax.optimization_barrier((near, mate_grads))
    mate_near = call(
        near_kernel, block(2 * PANEL), 0, [vmem] * 3, mate_grads, panels, across, name="mate",
    )
    far, mate_scores = call(
        far_kernel, (block(PANEL), block(2 * PANEL)), 0, [vmem] * 8,
        grads, mate_grads, near, mate_near, rest, *parts, name="far",
    )
    mate_scores = send(mate_scores, TO_CORE)
    return call(
        last_kernel, jax.ShapeDtypeStruct((1, DOC_OWN, 4 * PANEL), jnp.float32), 0,
        [vmem] * 4, panel_order, near, far, mate_scores, name="last",
    )


def solution(mesh):
    placed = (
        P("query", "docs", None),
        P("query", "docs", None),
        P(),
        P(),
        P("query", None),
        P("query", "docs", None),
        P("query", "docs", None),
        P("query", None, "docs"),
        P("docs", None),
    )
    return jax.shard_map(
        shards, mesh=mesh, in_specs=placed, out_specs=P("query", "docs", None), check_vma=False
    )
```

```python
import jax
import jax.numpy as jnp
from jax import lax
from jax.experimental import pallas as pl
from jax.experimental.pallas import tpu as pltpu
from jax.sharding import PartitionSpec as P

DOC_OWN = 8
R = 64
CAP = 4
DOCS = 64
TOK = 128
ROWS = DOCS * CAP
PANEL = 128
NT = (((1,), (1,)), ((), ()))
FIRST = 62


def spread_kernel(spread_ref):
    source = lax.broadcasted_iota(jnp.int32, (DOCS, ROWS), 0)
    place = lax.broadcasted_iota(jnp.int32, (DOCS, ROWS), 1) >> 2
    spread_ref[...] = jnp.where((place ^ FIRST) == source, 1.0, 0.0).astype(jnp.bfloat16)


def take_kernel(len_ref, own_ref, take_ref):
    lens = len_ref[...].astype(jnp.float32)
    owners = (own_ref[...] ^ FIRST).astype(jnp.float32)
    one = lax.broadcasted_iota(jnp.int32, (DOCS, DOCS), 0)
    other = lax.broadcasted_iota(jnp.int32, (DOCS, DOCS), 1)
    start = jnp.sum(jnp.where(other < one, lens, 0.0), axis=1, keepdims=True)
    size = jnp.sum(jnp.where(other == one, lens, 0.0), axis=1, keepdims=True)
    owner = jnp.sum(jnp.where(other == one, owners, 0.0), axis=1, keepdims=True)
    token = lax.broadcasted_iota(jnp.int32, (DOCS, TOK), 1).astype(jnp.float32)
    inside = (token >= start) & (token < start + size)
    goal = jnp.sum(jnp.where(inside, CAP * owner + token - start, 0.0), axis=0, keepdims=True)
    row = lax.broadcasted_iota(jnp.int32, (ROWS, TOK), 0).astype(jnp.float32)
    take_ref[...] = jnp.where(row == goal, 1.0, 0.0).astype(jnp.bfloat16)


def grad_kernel(grad_ref, wout_ref, low_ref):
    low_ref[...] = lax.dot_general(grad_ref[0], wout_ref[...], NT, preferred_element_type=jnp.float32)


def pack_kernel(act_ref, win_ref, take_ref, low_ref, rows_ref):
    act_low = lax.dot_general(act_ref[0], win_ref[...], NT, preferred_element_type=jnp.float32)
    rows = jnp.concatenate([low_ref[...], act_low], axis=1).astype(jnp.bfloat16)
    rows_ref[...] = jnp.dot(
        take_ref[...], rows, preferred_element_type=jnp.float32
    ).astype(jnp.bfloat16)


def project(activations, out_grads, proj_in, proj_out, lengths, piece_owner):
    vmem = pl.BlockSpec(memory_space=pltpu.VMEM)
    take = call(
        take_kernel, jax.ShapeDtypeStruct((ROWS, TOK), jnp.bfloat16), 0, [vmem] * 2,
        lengths, piece_owner, name="take",
    )
    grad_low = call(
        grad_kernel, jax.ShapeDtypeStruct((TOK, R), jnp.float32), 0, [vmem] * 2,
        out_grads, proj_out.T, name="grads",
    )
    return call(
        pack_kernel, jax.ShapeDtypeStruct((ROWS, 2 * R), jnp.bfloat16), 0, [vmem] * 4,
        activations, proj_in.T, take, grad_low, name="pack",
    )


def call(kernel, out_shape, cost_us, in_specs, *given, **more):
    return pl.pallas_call(
        kernel,
        out_shape=out_shape,
        in_specs=in_specs,
        out_specs=jax.tree.map(lambda _: pl.BlockSpec(memory_space=pltpu.VMEM), out_shape),
        compiler_params=pltpu.CompilerParams(vmem_limit_bytes=16 << 20),
        cost_estimate=pl.CostEstimate(
            flops=cost_us * 10**9, bytes_accessed=cost_us * 10**6, transcendentals=0
        ),
        **more,
    )(*given)


def document_kernel(slot_ref, spread_ref, rows_ref, panel_ref, grads_ref):
    doc = lax.broadcasted_iota(jnp.int32, (DOC_OWN, DOCS), 0)
    mine = jnp.where(slot_ref[...] == doc, 1.0, 0.0).astype(jnp.bfloat16)
    member = jnp.dot(mine, spread_ref[...], preferred_element_type=jnp.float32)

    rows = rows_ref[...]
    eye = (lax.broadcasted_iota(jnp.int32, (2 * R, 2 * R), 0)
           == lax.broadcasted_iota(jnp.int32, (2 * R, 2 * R), 1))
    eye = jnp.where(eye, 1.0, 0.0).astype(jnp.bfloat16)
    turned = lax.dot_general(eye, rows, NT, preferred_element_type=jnp.float32)
    masked = turned[:R][:, None, :] * member[None]
    masked = masked.reshape(R * DOC_OWN, ROWS).astype(jnp.bfloat16)
    wide = rows.astype(jnp.float32)
    lane = lax.broadcasted_iota(jnp.int32, (ROWS, 2 * R), 1)
    twice = jnp.where(lane < R, pltpu.roll(wide, R, 1), wide).astype(jnp.bfloat16)
    grads = jnp.dot(masked, twice, preferred_element_type=jnp.float32)
    grads = grads.reshape(R, DOC_OWN, 2 * R)
    low_half = lax.broadcasted_iota(jnp.int32, (DOC_OWN, 2 * R), 1) < R
    grads_ref[...] = jnp.concatenate(
        [jnp.where(low_half, grads[2 * i], grads[2 * i + 1]) for i in range(R // 2)], axis=1
    ).astype(jnp.bfloat16)


def near_kernel(grads_ref, own_ref, out_ref):
    out_ref[...] = lax.dot_general(
        grads_ref[...], own_ref[...], NT, preferred_element_type=jnp.float32
    )


def far_kernel(grads_ref, mate_grads_ref, own_ref, across_ref, out_ref, mate_out_ref):
    mate_grads = mate_grads_ref[...]
    mate_out_ref[:, :PANEL] = lax.dot_general(
        mate_grads, own_ref[...], NT, preferred_element_type=jnp.float32
    )
    both = jnp.concatenate([grads_ref[...], mate_grads], axis=0)
    both = lax.dot_general(both, across_ref[...], NT, preferred_element_type=jnp.float32)
    out_ref[...] = both[:DOC_OWN]
    mate_out_ref[:, PANEL:] = both[DOC_OWN:]


def last_kernel(order_ref, near_ref, far_ref, mate_ref, out_ref):
    query_at = lax.axis_index("query")

    blocks = [near_ref[...], mate_ref[:, :PANEL], far_ref[...], mate_ref[:, PANEL:]]
    for at in range(4):
        wanted = order_ref[:, at:at + 1]
        out_ref[0, :, at * PANEL:(at + 1) * PANEL] = sum(
            jnp.where(wanted == (query_at ^ kth), block, 0.0) for kth, block in enumerate(blocks)
        )


def hop(fn):
    pairs = []
    for z in range(8):
        for y in range(4):
            for x in range(4):
                for core in range(2):
                    at = []
                    for c in ((z, y, x, core), fn(z, y, x, core)):
                        at.append((((c[0] * 4 + c[1]) * 2 + c[2] % 2) * 2 + c[2] // 2) * 2 + c[3])
                    pairs.append(tuple(at))
    return pairs


TO_CORE = hop(lambda z, y, x, core: (z, y, x, 1 - core))
TO_CROSS = hop(lambda z, y, x, core: (z, y, 3 - x, core))


def send(value, pairs):
    return lax.ppermute(value, ("docs", "query"), pairs)


def shards(
    activations, out_grads, proj_in, proj_out, panels, lengths, piece_owner, doc_slot, panel_order
):
    vmem = pl.BlockSpec(memory_space=pltpu.VMEM)
    spread = call(
        spread_kernel, jax.ShapeDtypeStruct((DOCS, ROWS), jnp.bfloat16), 10, [], name="spread",
    )
    leaving, spread = lax.optimization_barrier((panels, spread))
    across = send(leaving, TO_CROSS)
    packed = project(activations, out_grads, proj_in, proj_out, lengths[0], piece_owner[0])
    arrived = lax.all_to_all(
        packed.reshape(DOCS, CAP, 2 * R), "docs", split_axis=0, concat_axis=0, tiled=True,
        axis_index_groups=[[place ^ FIRST for place in range(DOCS)]],
    ).reshape(ROWS, 2 * R)

    def block(width):
        return jax.ShapeDtypeStruct((DOC_OWN, width), jnp.float32)

    grads = call(
        document_kernel, jax.ShapeDtypeStruct((DOC_OWN, R * R), jnp.bfloat16), 0,
        [vmem] * 4, doc_slot[0].reshape(1, DOCS), spread, arrived, panels, name="documents",
    )
    mate_grads = send(grads, TO_CORE)
    near = call(near_kernel, block(PANEL), 0, [vmem] * 2, grads, panels, name="near")
    near, mate_grads = lax.optimization_barrier((near, mate_grads))
    far, mate_scores = call(
        far_kernel, (block(PANEL), block(2 * PANEL)), 0, [vmem] * 4,
        grads, mate_grads, panels, across, name="far",
    )
    mate_scores = send(mate_scores, TO_CORE)
    return call(
        last_kernel, jax.ShapeDtypeStruct((1, DOC_OWN, 4 * PANEL), jnp.float32), 0,
        [vmem] * 4, panel_order, near, far, mate_scores, name="last",
    )


def solution(mesh):
    placed = (
        P("query", "docs", None),
        P("query", "docs", None),
        P(),
        P(),
        P("query", None),
        P("query", "docs", None),
        P("query", "docs", None),
        P("query", None, "docs"),
        P("docs", None),
    )
    return jax.shard_map(
        shards, mesh=mesh, in_specs=placed, out_specs=P("query", "docs", None), check_vma=False
    )
```

```python
import jax
import jax.numpy as jnp
from jax import lax
from jax.experimental import pallas as pl
from jax.experimental.pallas import tpu as pltpu
from jax.sharding import PartitionSpec as P

DOC_OWN = 8
R = 64
CAP = 4
DOCS = 64
TOK = 128
ROWS = DOCS * CAP
PANEL = 128
NT = (((1,), (1,)), ((), ()))
FIRST = 62


def spread_kernel(spread_ref):
    source = lax.broadcasted_iota(jnp.int32, (DOCS, ROWS), 0)
    place = lax.broadcasted_iota(jnp.int32, (DOCS, ROWS), 1) >> 2
    spread_ref[...] = jnp.where((place ^ FIRST) == source, 1.0, 0.0).astype(jnp.bfloat16)


def take_kernel(len_ref, own_ref, take_ref):
    lens = len_ref[...].astype(jnp.float32)
    owners = (own_ref[...] ^ FIRST).astype(jnp.float32)
    one = lax.broadcasted_iota(jnp.int32, (DOCS, DOCS), 0)
    other = lax.broadcasted_iota(jnp.int32, (DOCS, DOCS), 1)
    start = jnp.sum(jnp.where(other < one, lens, 0.0), axis=1, keepdims=True)
    size = jnp.sum(jnp.where(other == one, lens, 0.0), axis=1, keepdims=True)
    owner = jnp.sum(jnp.where(other == one, owners, 0.0), axis=1, keepdims=True)
    token = lax.broadcasted_iota(jnp.int32, (DOCS, TOK), 1).astype(jnp.float32)
    inside = (token >= start) & (token < start + size)
    goal = jnp.sum(jnp.where(inside, CAP * owner + token - start, 0.0), axis=0, keepdims=True)
    row = lax.broadcasted_iota(jnp.int32, (ROWS, TOK), 0).astype(jnp.float32)
    take_ref[...] = jnp.where(row == goal, 1.0, 0.0).astype(jnp.bfloat16)


def grad_kernel(grad_ref, wout_ref, low_ref):
    low_ref[...] = lax.dot_general(grad_ref[0], wout_ref[...], NT, preferred_element_type=jnp.float32)


def pack_kernel(act_ref, win_ref, take_ref, low_ref, rows_ref):
    act_low = lax.dot_general(act_ref[0], win_ref[...], NT, preferred_element_type=jnp.float32)
    rows = jnp.concatenate([low_ref[...], act_low], axis=1).astype(jnp.bfloat16)
    rows_ref[...] = jnp.dot(
        take_ref[...], rows, preferred_element_type=jnp.float32
    ).astype(jnp.bfloat16)


def project(activations, out_grads, proj_in, proj_out, lengths, piece_owner):
    vmem = pl.BlockSpec(memory_space=pltpu.VMEM)
    take = call(
        take_kernel, jax.ShapeDtypeStruct((ROWS, TOK), jnp.bfloat16), 0, [vmem] * 2,
        lengths, piece_owner, name="take",
    )
    take, out_grads = lax.optimization_barrier((take, out_grads))
    grad_low = call(
        grad_kernel, jax.ShapeDtypeStruct((TOK, R), jnp.float32), 0, [vmem] * 2,
        out_grads, proj_out.T, name="grads",
    )
    return call(
        pack_kernel, jax.ShapeDtypeStruct((ROWS, 2 * R), jnp.bfloat16), 0, [vmem] * 4,
        activations, proj_in.T, take, grad_low, name="pack",
    )


def call(kernel, out_shape, cost_us, in_specs, *given, **more):
    return pl.pallas_call(
        kernel,
        out_shape=out_shape,
        in_specs=in_specs,
        out_specs=jax.tree.map(lambda _: pl.BlockSpec(memory_space=pltpu.VMEM), out_shape),
        compiler_params=pltpu.CompilerParams(vmem_limit_bytes=16 << 20),
        cost_estimate=pl.CostEstimate(
            flops=cost_us * 10**9, bytes_accessed=cost_us * 10**6, transcendentals=0
        ),
        **more,
    )(*given)


def document_kernel(slot_ref, spread_ref, rows_ref, panel_ref, grads_ref):
    doc = lax.broadcasted_iota(jnp.int32, (DOC_OWN, DOCS), 0)
    mine = jnp.where(slot_ref[...] == doc, 1.0, 0.0).astype(jnp.bfloat16)
    member = jnp.dot(mine, spread_ref[...], preferred_element_type=jnp.float32)

    rows = rows_ref[...]
    eye = (lax.broadcasted_iota(jnp.int32, (2 * R, 2 * R), 0)
           == lax.broadcasted_iota(jnp.int32, (2 * R, 2 * R), 1))
    eye = jnp.where(eye, 1.0, 0.0).astype(jnp.bfloat16)
    turned = lax.dot_general(eye, rows, NT, preferred_element_type=jnp.float32)
    masked = turned[:R][:, None, :] * member[None]
    masked = masked.reshape(R * DOC_OWN, ROWS).astype(jnp.bfloat16)
    wide = rows.astype(jnp.float32)
    lane = lax.broadcasted_iota(jnp.int32, (ROWS, 2 * R), 1)
    twice = jnp.where(lane < R, pltpu.roll(wide, R, 1), wide).astype(jnp.bfloat16)
    grads = jnp.dot(masked, twice, preferred_element_type=jnp.float32)
    grads = grads.reshape(R, DOC_OWN, 2 * R)
    low_half = lax.broadcasted_iota(jnp.int32, (DOC_OWN, 2 * R), 1) < R
    grads_ref[...] = jnp.concatenate(
        [jnp.where(low_half, grads[2 * i], grads[2 * i + 1]) for i in range(R // 2)], axis=1
    ).astype(jnp.bfloat16)


def near_kernel(grads_ref, own_ref, out_ref):
    out_ref[...] = lax.dot_general(
        grads_ref[...], own_ref[...], NT, preferred_element_type=jnp.float32
    )


def far_kernel(grads_ref, mate_grads_ref, mate_near_ref, across_ref, out_ref, mate_out_ref):
    mate_out_ref[:, :PANEL] = mate_near_ref[...]
    both = jnp.concatenate([grads_ref[...], mate_grads_ref[...]], axis=0)
    both = lax.dot_general(both, across_ref[...], NT, preferred_element_type=jnp.float32)
    out_ref[...] = both[:DOC_OWN]
    mate_out_ref[:, PANEL:] = both[DOC_OWN:]


def last_kernel(order_ref, near_ref, far_ref, mate_ref, out_ref):
    query_at = lax.axis_index("query")

    blocks = [near_ref[...], mate_ref[:, :PANEL], far_ref[...], mate_ref[:, PANEL:]]
    for at in range(4):
        wanted = order_ref[:, at:at + 1]
        out_ref[0, :, at * PANEL:(at + 1) * PANEL] = sum(
            jnp.where(wanted == (query_at ^ kth), block, 0.0) for kth, block in enumerate(blocks)
        )


def hop(fn):
    pairs = []
    for z in range(8):
        for y in range(4):
            for x in range(4):
                for core in range(2):
                    at = []
                    for c in ((z, y, x, core), fn(z, y, x, core)):
                        at.append((((c[0] * 4 + c[1]) * 2 + c[2] % 2) * 2 + c[2] // 2) * 2 + c[3])
                    pairs.append(tuple(at))
    return pairs


TO_CORE = hop(lambda z, y, x, core: (z, y, x, 1 - core))
TO_CROSS = hop(lambda z, y, x, core: (z, y, 3 - x, core))


def send(value, pairs):
    return lax.ppermute(value, ("docs", "query"), pairs)


def shards(
    activations, out_grads, proj_in, proj_out, panels, lengths, piece_owner, doc_slot, panel_order
):
    vmem = pl.BlockSpec(memory_space=pltpu.VMEM)
    spread = call(
        spread_kernel, jax.ShapeDtypeStruct((DOCS, ROWS), jnp.bfloat16), 3, [], name="spread",
    )
    across = send(panels, TO_CROSS)
    spread, proj_out = lax.optimization_barrier((spread, proj_out))
    packed = project(activations, out_grads, proj_in, proj_out, lengths[0], piece_owner[0])
    arrived = lax.all_to_all(
        packed.reshape(DOCS, CAP, 2 * R), "docs", split_axis=0, concat_axis=0, tiled=True,
        axis_index_groups=[[place ^ FIRST for place in range(DOCS)]],
    ).reshape(ROWS, 2 * R)

    def block(width):
        return jax.ShapeDtypeStruct((DOC_OWN, width), jnp.float32)

    grads = call(
        document_kernel, jax.ShapeDtypeStruct((DOC_OWN, R * R), jnp.bfloat16), 0,
        [vmem] * 4, doc_slot[0].reshape(1, DOCS), spread, arrived, panels, name="documents",
    )
    mate_grads = send(grads, TO_CORE)
    near = call(near_kernel, block(PANEL), 0, [vmem] * 2, grads, panels, name="near")
    near, mate_grads = lax.optimization_barrier((near, mate_grads))
    mate_near = call(near_kernel, block(PANEL), 0, [vmem] * 2, mate_grads, panels, name="mate")
    far, mate_scores = call(
        far_kernel, (block(PANEL), block(2 * PANEL)), 0, [vmem] * 4,
        grads, mate_grads, mate_near, across, name="far",
    )
    mate_scores = send(mate_scores, TO_CORE)
    return call(
        last_kernel, jax.ShapeDtypeStruct((1, DOC_OWN, 4 * PANEL), jnp.float32), 0,
        [vmem] * 4, panel_order, near, far, mate_scores, name="last",
    )


def solution(mesh):
    placed = (
        P("query", "docs", None),
        P("query", "docs", None),
        P(),
        P(),
        P("query", None),
        P("query", "docs", None),
        P("query", "docs", None),
        P("query", None, "docs"),
        P("docs", None),
    )
    return jax.shard_map(
        shards, mesh=mesh, in_specs=placed, out_specs=P("query", "docs", None), check_vma=False
    )
```

```python
import jax
import jax.numpy as jnp
from jax import lax
from jax.experimental import pallas as pl
from jax.experimental.pallas import tpu as pltpu
from jax.sharding import PartitionSpec as P

DOC_OWN = 8
R = 64
CAP = 4
DOCS = 64
TOK = 128
ROWS = DOCS * CAP
PANEL = 128
NT = (((1,), (1,)), ((), ()))
FIRST = 45


def spread_kernel(spread_ref):
    source = lax.broadcasted_iota(jnp.int32, (DOCS, ROWS), 0)
    place = lax.broadcasted_iota(jnp.int32, (DOCS, ROWS), 1) >> 2
    spread_ref[...] = jnp.where((place ^ FIRST) == source, 1.0, 0.0).astype(jnp.bfloat16)


def take_kernel(len_ref, own_ref, take_ref):
    lens = len_ref[...].astype(jnp.float32)
    owners = (own_ref[...] ^ FIRST).astype(jnp.float32)
    one = lax.broadcasted_iota(jnp.int32, (DOCS, DOCS), 0)
    other = lax.broadcasted_iota(jnp.int32, (DOCS, DOCS), 1)
    start = jnp.sum(jnp.where(other < one, lens, 0.0), axis=1, keepdims=True)
    size = jnp.sum(jnp.where(other == one, lens, 0.0), axis=1, keepdims=True)
    owner = jnp.sum(jnp.where(other == one, owners, 0.0), axis=1, keepdims=True)
    token = lax.broadcasted_iota(jnp.int32, (DOCS, TOK), 1).astype(jnp.float32)
    inside = (token >= start) & (token < start + size)
    goal = jnp.sum(jnp.where(inside, CAP * owner + token - start, 0.0), axis=0, keepdims=True)
    row = lax.broadcasted_iota(jnp.int32, (ROWS, TOK), 0).astype(jnp.float32)
    take_ref[...] = jnp.where(row == goal, 1.0, 0.0).astype(jnp.bfloat16)


def grad_kernel(grad_ref, wout_ref, low_ref):
    low_ref[...] = lax.dot_general(grad_ref[0], wout_ref[...], NT, preferred_element_type=jnp.float32)


def pack_kernel(act_ref, win_ref, take_ref, low_ref, rows_ref):
    act_low = lax.dot_general(act_ref[0], win_ref[...], NT, preferred_element_type=jnp.float32)
    rows = jnp.concatenate([low_ref[...], act_low], axis=1).astype(jnp.bfloat16)
    rows_ref[...] = jnp.dot(
        take_ref[...], rows, preferred_element_type=jnp.float32
    ).astype(jnp.bfloat16)


def project(activations, out_grads, proj_in, proj_out, lengths, piece_owner):
    vmem = pl.BlockSpec(memory_space=pltpu.VMEM)
    take = call(
        take_kernel, jax.ShapeDtypeStruct((ROWS, TOK), jnp.bfloat16), 0, [vmem] * 2,
        lengths, piece_owner, name="take",
    )
    take, out_grads = lax.optimization_barrier((take, out_grads))
    grad_low = call(
        grad_kernel, jax.ShapeDtypeStruct((TOK, R), jnp.float32), 0, [vmem] * 2,
        out_grads, proj_out.T, name="grads",
    )
    return call(
        pack_kernel, jax.ShapeDtypeStruct((ROWS, 2 * R), jnp.bfloat16), 0, [vmem] * 4,
        activations, proj_in.T, take, grad_low, name="pack",
    )


def call(kernel, out_shape, cost_us, in_specs, *given, **more):
    return pl.pallas_call(
        kernel,
        out_shape=out_shape,
        in_specs=in_specs,
        out_specs=jax.tree.map(lambda _: pl.BlockSpec(memory_space=pltpu.VMEM), out_shape),
        compiler_params=pltpu.CompilerParams(vmem_limit_bytes=16 << 20),
        cost_estimate=pl.CostEstimate(
            flops=cost_us * 10**9, bytes_accessed=cost_us * 10**6, transcendentals=0
        ),
        **more,
    )(*given)


def document_kernel(slot_ref, spread_ref, rows_ref, panel_ref, grads_ref):
    doc = lax.broadcasted_iota(jnp.int32, (DOC_OWN, DOCS), 0)
    mine = jnp.where(slot_ref[...] == doc, 1.0, 0.0).astype(jnp.bfloat16)
    member = jnp.dot(mine, spread_ref[...], preferred_element_type=jnp.float32)

    rows = rows_ref[...]
    eye = (lax.broadcasted_iota(jnp.int32, (2 * R, 2 * R), 0)
           == lax.broadcasted_iota(jnp.int32, (2 * R, 2 * R), 1))
    eye = jnp.where(eye, 1.0, 0.0).astype(jnp.bfloat16)
    turned = lax.dot_general(eye, rows, NT, preferred_element_type=jnp.float32)
    masked = turned[:R][:, None, :] * member[None]
    masked = masked.reshape(R * DOC_OWN, ROWS).astype(jnp.bfloat16)
    wide = rows.astype(jnp.float32)
    lane = lax.broadcasted_iota(jnp.int32, (ROWS, 2 * R), 1)
    twice = jnp.where(lane < R, pltpu.roll(wide, R, 1), wide).astype(jnp.bfloat16)
    grads = jnp.dot(masked, twice, preferred_element_type=jnp.float32)
    grads = grads.reshape(R, DOC_OWN, 2 * R)
    low_half = lax.broadcasted_iota(jnp.int32, (DOC_OWN, 2 * R), 1) < R
    grads_ref[...] = jnp.concatenate(
        [jnp.where(low_half, grads[2 * i], grads[2 * i + 1]) for i in range(R // 2)], axis=1
    ).astype(jnp.bfloat16)


def near_kernel(grads_ref, own_ref, out_ref):
    out_ref[...] = lax.dot_general(
        grads_ref[...], own_ref[...], NT, preferred_element_type=jnp.float32
    )


def far_kernel(grads_ref, mate_grads_ref, mate_near_ref, across_ref, out_ref, mate_out_ref):
    mate_out_ref[:, :PANEL] = mate_near_ref[...]
    both = jnp.concatenate([grads_ref[...], mate_grads_ref[...]], axis=0)
    both = lax.dot_general(both, across_ref[...], NT, preferred_element_type=jnp.float32)
    out_ref[...] = both[:DOC_OWN]
    mate_out_ref[:, PANEL:] = both[DOC_OWN:]


def last_kernel(order_ref, near_ref, far_ref, mate_ref, out_ref):
    query_at = lax.axis_index("query")

    blocks = [near_ref[...], mate_ref[:, :PANEL], far_ref[...], mate_ref[:, PANEL:]]
    for at in range(4):
        wanted = order_ref[:, at:at + 1]
        out_ref[0, :, at * PANEL:(at + 1) * PANEL] = sum(
            jnp.where(wanted == (query_at ^ kth), block, 0.0) for kth, block in enumerate(blocks)
        )


def hop(fn):
    pairs = []
    for z in range(8):
        for y in range(4):
            for x in range(4):
                for core in range(2):
                    at = []
                    for c in ((z, y, x, core), fn(z, y, x, core)):
                        at.append((((c[0] * 4 + c[1]) * 2 + c[2] % 2) * 2 + c[2] // 2) * 2 + c[3])
                    pairs.append(tuple(at))
    return pairs


TO_CORE = hop(lambda z, y, x, core: (z, y, x, 1 - core))
TO_CROSS = hop(lambda z, y, x, core: (z, y, 3 - x, core))


def send(value, pairs):
    return lax.ppermute(value, ("docs", "query"), pairs)


def shards(
    activations, out_grads, proj_in, proj_out, panels, lengths, piece_owner, doc_slot, panel_order
):
    vmem = pl.BlockSpec(memory_space=pltpu.VMEM)
    spread = call(
        spread_kernel, jax.ShapeDtypeStruct((DOCS, ROWS), jnp.bfloat16), 3, [], name="spread",
    )
    across = send(panels, TO_CROSS)
    spread, proj_out = lax.optimization_barrier((spread, proj_out))
    packed = project(activations, out_grads, proj_in, proj_out, lengths[0], piece_owner[0])
    arrived = lax.all_to_all(
        packed.reshape(DOCS, CAP, 2 * R), "docs", split_axis=0, concat_axis=0, tiled=True,
        axis_index_groups=[[place ^ FIRST for place in range(DOCS)]],
    ).reshape(ROWS, 2 * R)

    def block(width):
        return jax.ShapeDtypeStruct((DOC_OWN, width), jnp.float32)

    grads = call(
        document_kernel, jax.ShapeDtypeStruct((DOC_OWN, R * R), jnp.bfloat16), 0,
        [vmem] * 4, doc_slot[0].reshape(1, DOCS), spread, arrived, panels, name="documents",
    )
    mate_grads = send(grads, TO_CORE)
    near = call(near_kernel, block(PANEL), 0, [vmem] * 2, grads, panels, name="near")
    near, mate_grads = lax.optimization_barrier((near, mate_grads))
    mate_near = call(near_kernel, block(PANEL), 0, [vmem] * 2, mate_grads, panels, name="mate")
    far, mate_scores = call(
        far_kernel, (block(PANEL), block(2 * PANEL)), 0, [vmem] * 4,
        grads, mate_grads, mate_near, across, name="far",
    )
    mate_scores = send(mate_scores, TO_CORE)
    return call(
        last_kernel, jax.ShapeDtypeStruct((1, DOC_OWN, 4 * PANEL), jnp.float32), 0,
        [vmem] * 4, panel_order, near, far, mate_scores, name="last",
    )


def solution(mesh):
    placed = (
        P("query", "docs", None),
        P("query", "docs", None),
        P(),
        P(),
        P("query", None),
        P("query", "docs", None),
        P("query", "docs", None),
        P("query", None, "docs"),
        P("docs", None),
    )
    return jax.shard_map(
        shards, mesh=mesh, in_specs=placed, out_specs=P("query", "docs", None), check_vma=False
    )
```

```python
import jax
import jax.numpy as jnp
from jax import lax
from jax.experimental import pallas as pl
from jax.experimental.pallas import tpu as pltpu
from jax.sharding import PartitionSpec as P

DOC_OWN = 8
R = 64
CAP = 4
DOCS = 64
TOK = 128
ROWS = DOCS * CAP
PANEL = 128
NT = (((1,), (1,)), ((), ()))
FIRST = 37


def spread_kernel(spread_ref):
    source = lax.broadcasted_iota(jnp.int32, (DOCS, ROWS), 0)
    place = lax.broadcasted_iota(jnp.int32, (DOCS, ROWS), 1) >> 2
    spread_ref[...] = jnp.where((place ^ FIRST) == source, 1.0, 0.0).astype(jnp.bfloat16)


def take_kernel(len_ref, own_ref, take_ref):
    lens = len_ref[...].astype(jnp.float32)
    owners = (own_ref[...] ^ FIRST).astype(jnp.float32)
    one = lax.broadcasted_iota(jnp.int32, (DOCS, DOCS), 0)
    other = lax.broadcasted_iota(jnp.int32, (DOCS, DOCS), 1)
    start = jnp.sum(jnp.where(other < one, lens, 0.0), axis=1, keepdims=True)
    size = jnp.sum(jnp.where(other == one, lens, 0.0), axis=1, keepdims=True)
    owner = jnp.sum(jnp.where(other == one, owners, 0.0), axis=1, keepdims=True)
    token = lax.broadcasted_iota(jnp.int32, (DOCS, TOK), 1).astype(jnp.float32)
    inside = (token >= start) & (token < start + size)
    goal = jnp.sum(jnp.where(inside, CAP * owner + token - start, 0.0), axis=0, keepdims=True)
    row = lax.broadcasted_iota(jnp.int32, (ROWS, TOK), 0).astype(jnp.float32)
    take_ref[...] = jnp.where(row == goal, 1.0, 0.0).astype(jnp.bfloat16)


def grad_kernel(grad_ref, wout_ref, low_ref):
    low_ref[...] = lax.dot_general(grad_ref[0], wout_ref[...], NT, preferred_element_type=jnp.float32)


def pack_kernel(act_ref, win_ref, take_ref, low_ref, rows_ref):
    act_low = lax.dot_general(act_ref[0], win_ref[...], NT, preferred_element_type=jnp.float32)
    rows = jnp.concatenate([low_ref[...], act_low], axis=1).astype(jnp.bfloat16)
    rows_ref[...] = jnp.dot(
        take_ref[...], rows, preferred_element_type=jnp.float32
    ).astype(jnp.bfloat16)


def project(activations, out_grads, proj_in, proj_out, lengths, piece_owner):
    vmem = pl.BlockSpec(memory_space=pltpu.VMEM)
    take = call(
        take_kernel, jax.ShapeDtypeStruct((ROWS, TOK), jnp.bfloat16), 0, [vmem] * 2,
        lengths, piece_owner, name="take",
    )
    take, out_grads = lax.optimization_barrier((take, out_grads))
    grad_low = call(
        grad_kernel, jax.ShapeDtypeStruct((TOK, R), jnp.float32), 0, [vmem] * 2,
        out_grads, proj_out.T, name="grads",
    )
    return call(
        pack_kernel, jax.ShapeDtypeStruct((ROWS, 2 * R), jnp.bfloat16), 0, [vmem] * 4,
        activations, proj_in.T, take, grad_low, name="pack",
    )


def call(kernel, out_shape, cost_us, in_specs, *given, **more):
    return pl.pallas_call(
        kernel,
        out_shape=out_shape,
        in_specs=in_specs,
        out_specs=jax.tree.map(lambda _: pl.BlockSpec(memory_space=pltpu.VMEM), out_shape),
        compiler_params=pltpu.CompilerParams(vmem_limit_bytes=16 << 20),
        cost_estimate=pl.CostEstimate(
            flops=cost_us * 10**9, bytes_accessed=cost_us * 10**6, transcendentals=0
        ),
        **more,
    )(*given)


def document_kernel(slot_ref, spread_ref, rows_ref, panel_ref, grads_ref):
    doc = lax.broadcasted_iota(jnp.int32, (DOC_OWN, DOCS), 0)
    mine = jnp.where(slot_ref[...] == doc, 1.0, 0.0).astype(jnp.bfloat16)
    member = jnp.dot(mine, spread_ref[...], preferred_element_type=jnp.float32)

    rows = rows_ref[...]
    eye = (lax.broadcasted_iota(jnp.int32, (2 * R, 2 * R), 0)
           == lax.broadcasted_iota(jnp.int32, (2 * R, 2 * R), 1))
    eye = jnp.where(eye, 1.0, 0.0).astype(jnp.bfloat16)
    turned = lax.dot_general(eye, rows, NT, preferred_element_type=jnp.float32)
    masked = turned[:R][:, None, :] * member[None]
    masked = masked.reshape(R * DOC_OWN, ROWS).astype(jnp.bfloat16)
    wide = rows.astype(jnp.float32)
    lane = lax.broadcasted_iota(jnp.int32, (ROWS, 2 * R), 1)
    twice = jnp.where(lane < R, pltpu.roll(wide, R, 1), wide).astype(jnp.bfloat16)
    grads = jnp.dot(masked, twice, preferred_element_type=jnp.float32)
    grads = grads.reshape(R, DOC_OWN, 2 * R)
    low_half = lax.broadcasted_iota(jnp.int32, (DOC_OWN, 2 * R), 1) < R
    grads_ref[...] = jnp.concatenate(
        [jnp.where(low_half, grads[2 * i], grads[2 * i + 1]) for i in range(R // 2)], axis=1
    ).astype(jnp.bfloat16)


def near_kernel(grads_ref, own_ref, out_ref):
    out_ref[...] = lax.dot_general(
        grads_ref[...], own_ref[...], NT, preferred_element_type=jnp.float32
    )


def far_kernel(grads_ref, mate_grads_ref, mate_near_ref, across_ref, out_ref, mate_out_ref):
    mate_out_ref[:, :PANEL] = mate_near_ref[...]
    both = jnp.concatenate([grads_ref[...], mate_grads_ref[...]], axis=0)
    both = lax.dot_general(both, across_ref[...], NT, preferred_element_type=jnp.float32)
    out_ref[...] = both[:DOC_OWN]
    mate_out_ref[:, PANEL:] = both[DOC_OWN:]


def last_kernel(order_ref, near_ref, far_ref, mate_ref, out_ref):
    query_at = lax.axis_index("query")

    blocks = [near_ref[...], mate_ref[:, :PANEL], far_ref[...], mate_ref[:, PANEL:]]
    for at in range(4):
        wanted = order_ref[:, at:at + 1]
        out_ref[0, :, at * PANEL:(at + 1) * PANEL] = sum(
            jnp.where(wanted == (query_at ^ kth), block, 0.0) for kth, block in enumerate(blocks)
        )


def hop(fn):
    pairs = []
    for z in range(8):
        for y in range(4):
            for x in range(4):
                for core in range(2):
                    at = []
                    for c in ((z, y, x, core), fn(z, y, x, core)):
                        at.append((((c[0] * 4 + c[1]) * 2 + c[2] % 2) * 2 + c[2] // 2) * 2 + c[3])
                    pairs.append(tuple(at))
    return pairs


TO_CORE = hop(lambda z, y, x, core: (z, y, x, 1 - core))
TO_CROSS = hop(lambda z, y, x, core: (z, y, 3 - x, core))


def send(value, pairs):
    return lax.ppermute(value, ("docs", "query"), pairs)


def shards(
    activations, out_grads, proj_in, proj_out, panels, lengths, piece_owner, doc_slot, panel_order
):
    vmem = pl.BlockSpec(memory_space=pltpu.VMEM)
    spread = call(
        spread_kernel, jax.ShapeDtypeStruct((DOCS, ROWS), jnp.bfloat16), 3, [], name="spread",
    )
    across = send(panels, TO_CROSS)
    spread, proj_out = lax.optimization_barrier((spread, proj_out))
    packed = project(activations, out_grads, proj_in, proj_out, lengths[0], piece_owner[0])
    arrived = lax.all_to_all(
        packed.reshape(DOCS, CAP, 2 * R), "docs", split_axis=0, concat_axis=0, tiled=True,
        axis_index_groups=[[place ^ FIRST for place in range(DOCS)]],
    ).reshape(ROWS, 2 * R)

    def block(width):
        return jax.ShapeDtypeStruct((DOC_OWN, width), jnp.float32)

    grads = call(
        document_kernel, jax.ShapeDtypeStruct((DOC_OWN, R * R), jnp.bfloat16), 0,
        [vmem] * 4, doc_slot[0].reshape(1, DOCS), spread, arrived, panels, name="documents",
    )
    mate_grads = send(grads, TO_CORE)
    near = call(near_kernel, block(PANEL), 0, [vmem] * 2, grads, panels, name="near")
    near, mate_grads = lax.optimization_barrier((near, mate_grads))
    mate_near = call(near_kernel, block(PANEL), 0, [vmem] * 2, mate_grads, panels, name="mate")
    far, mate_scores = call(
        far_kernel, (block(PANEL), block(2 * PANEL)), 0, [vmem] * 4,
        grads, mate_grads, mate_near, across, name="far",
    )
    mate_scores = send(mate_scores, TO_CORE)
    return call(
        last_kernel, jax.ShapeDtypeStruct((1, DOC_OWN, 4 * PANEL), jnp.float32), 0,
        [vmem] * 4, panel_order, near, far, mate_scores, name="last",
    )


def solution(mesh):
    placed = (
        P("query", "docs", None),
        P("query", "docs", None),
        P(),
        P(),
        P("query", None),
        P("query", "docs", None),
        P("query", "docs", None),
        P("query", None, "docs"),
        P("docs", None),
    )
    return jax.shard_map(
        shards, mesh=mesh, in_specs=placed, out_specs=P("query", "docs", None), check_vma=False
    )
```

```python
import jax
import jax.numpy as jnp
from jax import lax
from jax.experimental import pallas as pl
from jax.experimental.pallas import tpu as pltpu
from jax.sharding import PartitionSpec as P

DOC_OWN = 8
R = 64
CAP = 4
DOCS = 64
TOK = 128
ROWS = DOCS * CAP
PANEL = 128
NT = (((1,), (1,)), ((), ()))
FIRST = 36


def spread_kernel(spread_ref):
    source = lax.broadcasted_iota(jnp.int32, (DOCS, ROWS), 0)
    place = lax.broadcasted_iota(jnp.int32, (DOCS, ROWS), 1) >> 2
    spread_ref[...] = jnp.where((place ^ FIRST) == source, 1.0, 0.0).astype(jnp.bfloat16)


def take_kernel(len_ref, own_ref, take_ref):
    lens = len_ref[...].astype(jnp.float32)
    owners = (own_ref[...] ^ FIRST).astype(jnp.float32)
    one = lax.broadcasted_iota(jnp.int32, (DOCS, DOCS), 0)
    other = lax.broadcasted_iota(jnp.int32, (DOCS, DOCS), 1)
    start = jnp.sum(jnp.where(other < one, lens, 0.0), axis=1, keepdims=True)
    size = jnp.sum(jnp.where(other == one, lens, 0.0), axis=1, keepdims=True)
    owner = jnp.sum(jnp.where(other == one, owners, 0.0), axis=1, keepdims=True)
    token = lax.broadcasted_iota(jnp.int32, (DOCS, TOK), 1).astype(jnp.float32)
    inside = (token >= start) & (token < start + size)
    goal = jnp.sum(jnp.where(inside, CAP * owner + token - start, 0.0), axis=0, keepdims=True)
    row = lax.broadcasted_iota(jnp.int32, (ROWS, TOK), 0).astype(jnp.float32)
    take_ref[...] = jnp.where(row == goal, 1.0, 0.0).astype(jnp.bfloat16)


def grad_kernel(grad_ref, wout_ref, low_ref):
    low_ref[...] = lax.dot_general(grad_ref[0], wout_ref[...], NT, preferred_element_type=jnp.float32)


def pack_kernel(act_ref, win_ref, take_ref, low_ref, rows_ref):
    act_low = lax.dot_general(act_ref[0], win_ref[...], NT, preferred_element_type=jnp.float32)
    rows = jnp.concatenate([low_ref[...], act_low], axis=1).astype(jnp.bfloat16)
    rows_ref[...] = jnp.dot(
        take_ref[...], rows, preferred_element_type=jnp.float32
    ).astype(jnp.bfloat16)


def project(activations, out_grads, proj_in, proj_out, lengths, piece_owner):
    vmem = pl.BlockSpec(memory_space=pltpu.VMEM)
    take = call(
        take_kernel, jax.ShapeDtypeStruct((ROWS, TOK), jnp.bfloat16), 0, [vmem] * 2,
        lengths, piece_owner, name="take",
    )
    take, out_grads = lax.optimization_barrier((take, out_grads))
    grad_low = call(
        grad_kernel, jax.ShapeDtypeStruct((TOK, R), jnp.float32), 0, [vmem] * 2,
        out_grads, proj_out.T, name="grads",
    )
    return call(
        pack_kernel, jax.ShapeDtypeStruct((ROWS, 2 * R), jnp.bfloat16), 0, [vmem] * 4,
        activations, proj_in.T, take, grad_low, name="pack",
    )


def call(kernel, out_shape, cost_us, in_specs, *given, **more):
    return pl.pallas_call(
        kernel,
        out_shape=out_shape,
        in_specs=in_specs,
        out_specs=jax.tree.map(lambda _: pl.BlockSpec(memory_space=pltpu.VMEM), out_shape),
        compiler_params=pltpu.CompilerParams(vmem_limit_bytes=16 << 20),
        cost_estimate=pl.CostEstimate(
            flops=cost_us * 10**9, bytes_accessed=cost_us * 10**6, transcendentals=0
        ),
        **more,
    )(*given)


def document_kernel(slot_ref, spread_ref, rows_ref, panel_ref, grads_ref):
    doc = lax.broadcasted_iota(jnp.int32, (DOC_OWN, DOCS), 0)
    mine = jnp.where(slot_ref[...] == doc, 1.0, 0.0).astype(jnp.bfloat16)
    member = jnp.dot(mine, spread_ref[...], preferred_element_type=jnp.float32)

    rows = rows_ref[...]
    eye = (lax.broadcasted_iota(jnp.int32, (2 * R, 2 * R), 0)
           == lax.broadcasted_iota(jnp.int32, (2 * R, 2 * R), 1))
    eye = jnp.where(eye, 1.0, 0.0).astype(jnp.bfloat16)
    turned = lax.dot_general(eye, rows, NT, preferred_element_type=jnp.float32)
    masked = turned[:R][:, None, :] * member[None]
    masked = masked.reshape(R * DOC_OWN, ROWS).astype(jnp.bfloat16)
    wide = rows.astype(jnp.float32)
    lane = lax.broadcasted_iota(jnp.int32, (ROWS, 2 * R), 1)
    twice = jnp.where(lane < R, pltpu.roll(wide, R, 1), wide).astype(jnp.bfloat16)
    grads = jnp.dot(masked, twice, preferred_element_type=jnp.float32)
    grads = grads.reshape(R, DOC_OWN, 2 * R)
    low_half = lax.broadcasted_iota(jnp.int32, (DOC_OWN, 2 * R), 1) < R
    grads_ref[...] = jnp.concatenate(
        [jnp.where(low_half, grads[2 * i], grads[2 * i + 1]) for i in range(R // 2)], axis=1
    ).astype(jnp.bfloat16)


def near_kernel(grads_ref, own_ref, out_ref):
    out_ref[...] = lax.dot_general(
        grads_ref[...], own_ref[...], NT, preferred_element_type=jnp.float32
    )


def far_kernel(grads_ref, mate_grads_ref, mate_near_ref, across_ref, out_ref, mate_out_ref):
    mate_out_ref[:, :PANEL] = mate_near_ref[...]
    both = jnp.concatenate([grads_ref[...], mate_grads_ref[...]], axis=0)
    both = lax.dot_general(both, across_ref[...], NT, preferred_element_type=jnp.float32)
    out_ref[...] = both[:DOC_OWN]
    mate_out_ref[:, PANEL:] = both[DOC_OWN:]


def last_kernel(order_ref, near_ref, far_ref, mate_ref, out_ref):
    query_at = lax.axis_index("query")

    blocks = [near_ref[...], mate_ref[:, :PANEL], far_ref[...], mate_ref[:, PANEL:]]
    for at in range(4):
        wanted = order_ref[:, at:at + 1]
        out_ref[0, :, at * PANEL:(at + 1) * PANEL] = sum(
            jnp.where(wanted == (query_at ^ kth), block, 0.0) for kth, block in enumerate(blocks)
        )


def hop(fn):
    pairs = []
    for z in range(8):
        for y in range(4):
            for x in range(4):
                for core in range(2):
                    at = []
                    for c in ((z, y, x, core), fn(z, y, x, core)):
                        at.append((((c[0] * 4 + c[1]) * 2 + c[2] % 2) * 2 + c[2] // 2) * 2 + c[3])
                    pairs.append(tuple(at))
    return pairs


TO_CORE = hop(lambda z, y, x, core: (z, y, x, 1 - core))
TO_CROSS = hop(lambda z, y, x, core: (z, y, 3 - x, core))


def send(value, pairs):
    return lax.ppermute(value, ("docs", "query"), pairs)


def shards(
    activations, out_grads, proj_in, proj_out, panels, lengths, piece_owner, doc_slot, panel_order
):
    vmem = pl.BlockSpec(memory_space=pltpu.VMEM)
    spread = call(
        spread_kernel, jax.ShapeDtypeStruct((DOCS, ROWS), jnp.bfloat16), 3, [], name="spread",
    )
    across = send(panels, TO_CROSS)
    spread, proj_out = lax.optimization_barrier((spread, proj_out))
    packed = project(activations, out_grads, proj_in, proj_out, lengths[0], piece_owner[0])
    arrived = lax.all_to_all(
        packed.reshape(DOCS, CAP, 2 * R), "docs", split_axis=0, concat_axis=0, tiled=True,
        axis_index_groups=[[place ^ FIRST for place in range(DOCS)]],
    ).reshape(ROWS, 2 * R)

    def block(width):
        return jax.ShapeDtypeStruct((DOC_OWN, width), jnp.float32)

    grads = call(
        document_kernel, jax.ShapeDtypeStruct((DOC_OWN, R * R), jnp.bfloat16), 0,
        [vmem] * 4, doc_slot[0].reshape(1, DOCS), spread, arrived, panels, name="documents",
    )
    mate_grads = send(grads, TO_CORE)
    near = call(near_kernel, block(PANEL), 0, [vmem] * 2, grads, panels, name="near")
    near, mate_grads = lax.optimization_barrier((near, mate_grads))
    mate_near = call(near_kernel, block(PANEL), 0, [vmem] * 2, mate_grads, panels, name="mate")
    far, mate_scores = call(
        far_kernel, (block(PANEL), block(2 * PANEL)), 0, [vmem] * 4,
        grads, mate_grads, mate_near, across, name="far",
    )
    mate_scores = send(mate_scores, TO_CORE)
    return call(
        last_kernel, jax.ShapeDtypeStruct((1, DOC_OWN, 4 * PANEL), jnp.float32), 0,
        [vmem] * 4, panel_order, near, far, mate_scores, name="last",
    )


def solution(mesh):
    placed = (
        P("query", "docs", None),
        P("query", "docs", None),
        P(),
        P(),
        P("query", None),
        P("query", "docs", None),
        P("query", "docs", None),
        P("query", None, "docs"),
        P("docs", None),
    )
    return jax.shard_map(
        shards, mesh=mesh, in_specs=placed, out_specs=P("query", "docs", None), check_vma=False
    )
```
